32 devices in a mesh: dp: 8 (over z, x), mp: 4 (over y, core).
Axes of the slice: x: 2, y: 2, z: 4, core: 2. Of those that a mesh axis runs over, the one named last changes fastest.
Arguments:
- images: bfloat16 [256, 196, 768], P('dp', None, 'mp'), may hold values from -6 to 6
- counts: int32 [8], P('dp'), may hold values from 8 to 32, as said below
- pre_gain: float32 [768], replicated, may hold values from 0.5 to 1.5
- pre_bias: float32 [768], replicated, may hold values from -3 to 3
- token_up: bfloat16 [196, 384], replicated, may hold values from -0.4375 to 0.4375
- token_up_bias: float32 [384], replicated, may hold values from -3 to 3
- token_down: bfloat16 [384, 196], replicated, may hold values from -0.4375 to 0.4375
- token_down_bias: float32 [196], replicated, may hold values from -3 to 3
- mid_gain: float32 [768], replicated, may hold values from 0.5 to 1.5
- mid_bias: float32 [768], replicated, may hold values from -3 to 3
- channel_up: bfloat16 [768, 3072], replicated, may hold values from -0.21875 to 0.21875
- channel_up_bias: float32 [3072], replicated, may hold values from -3 to 3
- channel_down: bfloat16 [3072, 768], replicated, may hold values from -0.15625 to 0.15625
- channel_down_bias: float32 [768], replicated, may hold values from -3 to 3
- cotangent: bfloat16 [256, 196, 768], P('dp', 'mp'), may hold values from -6 to 6
Outputs:
- block_out: bfloat16 [256, 196, 768], P('dp', 'mp')
- grad_images: bfloat16 [256, 196, 768], P('dp', None, 'mp')
- grad_pre_gain: float32 [768], replicated
- grad_pre_bias: float32 [768], replicated
- grad_token_up: float32 [196, 384], replicated
- grad_token_up_bias: float32 [384], replicated
- grad_token_down: float32 [384, 196], replicated
- grad_token_down_bias: float32 [196], replicated
- grad_mid_gain: float32 [768], replicated
- grad_mid_bias: float32 [768], replicated
- grad_channel_up: float32 [768, 3072], P(None, ('dp', 'mp'))
- grad_channel_up_bias: float32 [3072], replicated
- grad_channel_down: float32 [3072, 768], P(('dp', 'mp'))
- grad_channel_down_bias: float32 [768], replicated
The draws below stay inside these ranges and needn't reach their ends.
Inputs may be any that keep to these rules, and one draw needn't show every extreme that they name: `counts`: images present in a group; at least one group holds exactly 32.
All inputs are finite; a program needn't handle non-finite values.
Results may differ from the reference program's by a relative error of at most 0.0079.
Values may be sent and summed in bfloat16 or wider, within the bound.
A program may use at most 192 MiB of HBM per device.

```python
import jax
import jax.numpy as jnp
from jax import lax

D = 768
P_SIZE = 196
S = 384
DC = 3072
IMG = 32
B = 256
N_DP = 8


def draw_counts(key, part):
    key = jax.random.fold_in(key, 11)
    first, second = jax.random.split(key)
    values = jax.random.randint(first, (N_DP,), max(1, IMG // 4), IMG + 1).astype(jnp.int32)
    fullest = jax.random.randint(second, (), 0, N_DP)
    return values.at[fullest].set(IMG)


def level_of(stream_key, dims, cuts, low, largest):
    def one(dim, shards_of):
        heights = jax.random.uniform(jax.random.fold_in(jax.random.fold_in(stream_key, 6), dim), (shards_of,), jnp.float32, low / len(cuts), largest / len(cuts))
        return jnp.repeat(jnp.exp(heights), dims[dim] // shards_of).reshape((-1,) + (1,) * (len(dims) - dim - 1))

    factor_of = one(*cuts[0])
    for cut in cuts[1:]:
        factor_of = factor_of * one(*cut)
    return factor_of


def gaussian(key, extent, width, limit, pieces=(), kind=jnp.bfloat16):
    drawn = jax.random.normal(key, extent, jnp.float32) * width
    if len(pieces) > 0:
        drawn = level_of(key, extent, pieces, -0.22, 0.18) * drawn
    return jnp.clip(drawn, min=-limit, max=limit).astype(kind)


def setup_inputs(seed: int = 0) -> dict:
    keys = jax.random.split(jax.random.key(seed), 16)
    return {
        "images": gaussian(keys[0], (B, P_SIZE, D), 1.0, 6.0, ((0, 8), (2, 4))),
        "counts": draw_counts(jax.random.fold_in(keys[15], 71), 0),
        "pre_gain": jnp.clip(jax.random.uniform(keys[2], (D,), jnp.float32, 0.5, 1.5), 0.5, 1.5),
        "pre_bias": gaussian(keys[3], (D,), 0.5, 3.0, (), jnp.float32),
        "token_up": gaussian(keys[4], (P_SIZE, S), P_SIZE ** -0.5, 0.4375),
        "token_up_bias": gaussian(keys[5], (S,), 0.5, 3.0, (), jnp.float32),
        "token_down": gaussian(keys[6], (S, P_SIZE), (S // 2) ** -0.5, 0.4375),
        "token_down_bias": gaussian(keys[7], (P_SIZE,), 0.5, 3.0, (), jnp.float32),
        "mid_gain": jnp.clip(jax.random.uniform(keys[8], (D,), jnp.float32, 0.5, 1.5), 0.5, 1.5),
        "mid_bias": gaussian(keys[9], (D,), 0.5, 3.0, (), jnp.float32),
        "channel_up": gaussian(keys[10], (D, DC), D ** -0.5, 0.21875),
        "channel_up_bias": gaussian(keys[11], (DC,), 0.5, 3.0, (), jnp.float32),
        "channel_down": gaussian(keys[12], (DC, D), (DC // 2) ** -0.5, 0.15625),
        "channel_down_bias": gaussian(keys[13], (D,), 0.5, 3.0, (), jnp.float32),
        "cotangent": gaussian(keys[14], (B, P_SIZE, D), 1.0, 6.0, ((0, 8), (1, 4))),
    }


EPSILON = 1e-06
HIGH = lax.Precision.HIGHEST

@jax.custom_vjp
def low(v):
    return lax.optimization_barrier(v.astype(jnp.bfloat16)).astype(jnp.float32)

@jax.custom_vjp
def low_back(v):
    return v

def low_keep(v):
    return (low(v), None)

def low_pass(kept, grad):
    return (grad,)

def back_keep(v):
    return (v, None)

def back_low(kept, grad):
    return (low(grad),)
low.defvjp(low_keep, low_pass)
low_back.defvjp(back_keep, back_low)

def layer_norm(value, gain, bias):
    center = value - lax.optimization_barrier(jnp.mean(value, axis=-1, keepdims=True))
    spread = lax.optimization_barrier(jnp.mean(center * center, axis=-1, keepdims=True))
    return center * lax.rsqrt(spread + EPSILON) * gain + bias

def block(floats, pre_gain, pre_bias, token_up, token_up_bias, token_down, token_down_bias, mid_gain, mid_bias, channel_up, channel_up_bias, channel_down, channel_down_bias, valid):
    normed = low(layer_norm(floats, pre_gain, pre_bias))
    mixed_pre = low_back(jnp.einsum('npd,ps->nsd', normed, token_up, precision=HIGH) + token_up_bias[None, :, None])
    mixed = low(jax.nn.gelu(mixed_pre))
    token_out = jnp.einsum('nsd,sp->npd', mixed, token_down, precision=HIGH) + token_down_bias[None, :, None]
    middle = low(low_back(floats + token_out))
    normed2 = low(layer_norm(middle, mid_gain, mid_bias))
    hidden_pre = low_back(jnp.einsum('npd,df->npf', normed2, channel_up, precision=HIGH) + channel_up_bias)
    hidden = low(jax.nn.gelu(hidden_pre))
    channel_out = jnp.einsum('npf,fd->npd', hidden, channel_down, precision=HIGH) + channel_down_bias
    return valid[:, None, None] * (middle + channel_out)

def reference(images, counts, pre_gain, pre_bias, token_up, token_up_bias, token_down, token_down_bias, mid_gain, mid_bias, channel_up, channel_up_bias, channel_down, channel_down_bias, cotangent):
    weights = tuple((w.astype(jnp.float32) for w in (pre_gain, pre_bias, token_up, token_up_bias, token_down, token_down_bias, mid_gain, mid_bias, channel_up, channel_up_bias, channel_down, channel_down_bias)))
    grouped = images.reshape(N_DP, IMG, P_SIZE, D)
    grouped_cot = cotangent.reshape(N_DP, IMG, P_SIZE, D)

    def step(carry, item):
        group_images, group_cot, count = item
        valid = (jnp.arange(IMG, dtype=jnp.int32) < count).astype(jnp.float32)

        def forward(floats, *params):
            return block(floats, *params, valid)
        result, pull = jax.vjp(forward, group_images.astype(jnp.float32), *weights)
        grads = pull(group_cot.astype(jnp.float32))
        summed = tuple((c + g for c, g in zip(carry, grads[1:])))
        return (summed, (result.astype(jnp.bfloat16), grads[0].astype(jnp.bfloat16)))
    start = tuple((jnp.zeros_like(w) for w in weights))
    totals, (outs, grad_in) = lax.scan(step, start, (grouped, grouped_cot, counts))
    return (outs.reshape(B, P_SIZE, D), grad_in.reshape(B, P_SIZE, D), totals[0], totals[1], totals[2], totals[3], totals[4], totals[5], totals[6], totals[7], totals[8], totals[9], totals[10], totals[11])
```

```python
import functools

import jax
import jax.numpy as jnp
from jax import lax
from jax.experimental import pallas as pl
from jax.experimental.pallas import tpu as pltpu
from jax.sharding import PartitionSpec as P

EPSILON = 1e-06
GELU_ROOT = 0.7978845608028654
GELU_CUBE = 0.044715
BF = jnp.bfloat16
F32 = jnp.float32
HALF = 64
SUB = 8


def dot(left, right, left_dim=1, right_dim=0):
    return lax.dot_general(
        left, right, (((left_dim,), (right_dim,)), ((), ())), preferred_element_type=F32
    )


def gelu_parts(x):
    squares = x * x
    slope = squares * (GELU_ROOT * GELU_CUBE) + GELU_ROOT
    t = jnp.tanh(x * slope)
    half = 0.5 * x
    value = half + half * t
    inner = slope + squares * (2.0 * GELU_ROOT * GELU_CUBE)
    back = (0.5 + 0.5 * t) + (half * inner) * (1.0 - t * t)
    return value, back


def kernel(
    axes,
    counts, img_hbm, cot_hbm, cu_hbm, cd_hbm, tu, td, tub, tdb, g1, b1, mg, mb, cub, cdb,
    bo_hbm, gi_hbm, gch_hbm, small, gpre,
    img, cu, cd, gout, stat_out, stat_in, mean_inv, mixed_all, back_all, stage, send, frecv,
    mid, n2, hid, dpre, dn_acc, gbuf, acc_g, acc_b, gtu, gtd, up_bias,
    load_sem, out_sem, stat_send, stat_recv, f_send, f_recv, b_send, b_recv, credit,
):
    n_dp, n_mp = axes
    me = lax.axis_index("mp")
    images, local, patches = img.shape
    chunk = images // 2
    pairs = chunk // 2
    width = n_mp * local
    quarter = patches // n_mp
    qrows = quarter * SUB
    half_p = patches // 2
    blocks = cu.shape[1] // width
    odd = lax.rem(me, 2)

    def peer(step):
        return lax.rem(me + step, n_mp)

    barrier = pltpu.get_barrier_semaphore()
    for step in range(1, n_mp):
        pl.semaphore_signal(barrier, 1, device_id={"mp": peer(step)}, device_id_type=pl.DeviceIdType.MESH)

    loads = [
        pltpu.make_async_copy(img_hbm, img, load_sem.at[0]),
        pltpu.make_async_copy(cd_hbm, cd, load_sem.at[1]),
        pltpu.make_async_copy(cot_hbm.at[:, pl.ds(0, chunk)], gout.at[0], load_sem.at[2]),
        pltpu.make_async_copy(cot_hbm.at[:, pl.ds(chunk, chunk)], gout.at[1], load_sem.at[3]),
        pltpu.make_async_copy(cu_hbm, cu, load_sem.at[4]),
    ]
    for load in loads:
        load.start()

    loads[0].wait()

    @pl.loop(0, images)
    def _(b):
        x = img[b].astype(F32)
        total = jnp.sum(x, 0, keepdims=True)
        center = x - total * (1.0 / local)
        stat_out[pl.ds(b, 1), :] = total
        stat_out[pl.ds(images + b, 1), :] = jnp.sum(center * center, 0, keepdims=True)

    def stat_copy(phase, step):
        return pltpu.make_async_remote_copy(
            src_ref=stat_out, dst_ref=stat_in.at[phase, me],
            send_sem=stat_send.at[phase, step - 1], recv_sem=stat_recv.at[phase, step - 1],
            device_id={"mp": peer(step)}, device_id_type=pl.DeviceIdType.MESH,
        )

    def share_stats(phase):
        stat_in[phase, me] = stat_out[...]
        for step in (2, 1, 3):
            stat_copy(phase, step).start()

    def wait_stats(phase):
        for step in range(1, n_mp):
            stat_copy(phase, step).wait()

    pl.semaphore_wait(barrier, n_mp - 1)
    share_stats(0)

    row = lax.broadcasted_iota(jnp.int32, (chunk, width), 0)
    for load in loads[2:4]:
        load.wait()

    def valid_of(h):
        return jnp.where(row + h * chunk < counts[0], 1.0, 0.0)[None]

    down_bias = jnp.zeros((chunk, width), F32)
    for h in range(2):
        masked = gout[h].astype(F32) * valid_of(h)
        gout[h] = masked.astype(BF)
        down_bias = down_bias + jnp.sum(masked, 0)
    down_bias = jnp.sum(down_bias, 0, keepdims=True)

    wait_stats(0)
    sums = [stat_in[0, k] for k in range(n_mp)]
    mean = sum(s[:images] for s in sums) * (1.0 / width)
    square = sum(s[images:] for s in sums)
    for s in sums:
        gap = s[:images] * (1.0 / local) - mean
        square = square + float(local) * (gap * gap)
    mean_inv[0] = mean
    mean_inv[1] = lax.rsqrt(square * (1.0 / width) + EPSILON)

    eye = jnp.where(
        lax.broadcasted_iota(jnp.int32, (patches, patches), 0)
        == lax.broadcasted_iota(jnp.int32, (patches, patches), 1), 1.0, 0.0,
    ).astype(BF)

    def lanes(ref):
        tile = ref[...]
        return jnp.concatenate([tile, tile], 1)[:, :patches]

    gain_one, bias_one = lanes(g1), lanes(b1)
    token_down_bias = jnp.concatenate([tdb[...]] * 3, 1)

    def norm_of(b):
        return (img[b].astype(F32) - mean_inv[0, pl.ds(b, 1), :]) * mean_inv[1, pl.ds(b, 1), :]

    def slot_blocks(place):
        even = (0, 1, 2, 5, 3, 4)[place]
        other = (1, 2, 3, 0, 4, 5)[place]
        return even + odd * (other - even)

    def slot_rows(ref, q):
        rows = []
        for place in range(6):
            start = pl.multiple_of(slot_blocks(place) * HALF, HALF)
            rows.append(ref[q, pl.ds(start, HALF), :])
        return jnp.concatenate(rows, 0)

    def slot_images(b):
        rows = []
        for place in range(6):
            block = slot_blocks(place)
            which = block // 3
            start = pl.multiple_of((block - 3 * which) * HALF, HALF)
            rows.append(img[b + pairs * which, pl.ds(start, HALF), :])
        return jnp.concatenate(rows, 0)

    def forward_copy(h, step):
        return pltpu.make_async_remote_copy(
            src_ref=send.at[h, peer(step)], dst_ref=frecv.at[h, me],
            send_sem=f_send.at[h, step - 1], recv_sem=f_recv.at[h, step - 1],
            device_id={"mp": peer(step)}, device_id_type=pl.DeviceIdType.MESH,
        )

    def backward_copy(h, step):
        return pltpu.make_async_remote_copy(
            src_ref=send.at[h, peer(step)], dst_ref=frecv.at[h, me],
            send_sem=b_send.at[h, step - 1], recv_sem=b_recv.at[h, step - 1],
            device_id={"mp": peer(step)}, device_id_type=pl.DeviceIdType.MESH,
        )

    def token_forward(h):
        @pl.loop(0, pairs)
        def _(j):
            b = h * chunk + j
            q = h * pairs + j
            normed = jnp.concatenate(
                [(norm_of(b + e * pairs) * gain_one + bias_one).astype(BF) for e in range(2)], 0
            )
            value, back = gelu_parts(dot(normed, tu[...]) + tub[...])
            mixed_all[q] = value.astype(BF)
            back_all[q] = back.astype(BF)
            out = dot(td[...], slot_rows(mixed_all, q), 1, 1)
            out = out + dot(eye, slot_images(b), 1, 1) + token_down_bias
            for t in range(3):
                for side in range(2):
                    part = out[side * half_p : (side + 1) * half_p, t * 128 : (t + 1) * 128]
                    stage[2 * t + side, pl.ds(j, half_p, stride=SUB), :] = part

        for k in range(n_mp):
            for t in range(3):
                low_row = (k % 2) * qrows
                part = stage[2 * t + k // 2, low_row : low_row + qrows, :]
                send[h, k, :qrows, t * 128 : (t + 1) * 128] = part.astype(BF)
        frecv[h, me] = send[h, me]
        for step in (2, 1, 3):
            forward_copy(h, step).start()

    token_forward(0)
    token_forward(1)

    low_half = lax.broadcasted_iota(jnp.int32, (1, 1, 128), 2) < HALF
    tiles = [(12 * i, 12) for i in range(quarter // 12)]
    tiles += [(12 * (quarter // 12), quarter % 12)] if quarter % 12 else []

    def arrived(ref, h, k, start, count):
        padded = count + count % 2
        rows = ref[h, k, start * SUB : (start + padded) * SUB, :].astype(F32)
        return rows[: count * SUB].reshape(count, SUB, 3 * 128)

    def tile(array, i):
        return array[:, :, i * 128 : (i + 1) * 128]

    def swap(array):
        count = array.shape[0]
        return pltpu.roll(array.reshape(count * SUB, 128), HALF, 1).reshape(count, SUB, 128)

    def merge(h, start, count):
        parts = [arrived(frecv, h, k, start, count) for k in range(n_mp)]
        first, second = [], []
        for k in range(0, n_mp, 2):
            a, b = parts[k], parts[k + 1]
            first += [tile(a, 0), jnp.where(low_half, tile(a, 1), tile(b, 1)), tile(b, 0)]
            second += [tile(a, 2), swap(jnp.where(low_half, tile(b, 1), tile(a, 1))), tile(b, 2)]
        rows = jnp.stack([jnp.concatenate(first, 2), jnp.concatenate(second, 2)], 1)
        return rows.reshape(count * 2 * SUB, width)

    def centered(x):
        center = x - jnp.sum(x, 1, keepdims=True) * (1.0 / width)
        spread_two = jnp.sum(center * center, 1, keepdims=True) * (1.0 / width)
        return center, lax.rsqrt(spread_two + EPSILON)

    def layer_norm_two(h):
        for start, count in tiles:
            rows = pl.ds(start * chunk, count * chunk)
            x = merge(h, start, count)
            mid[rows, :] = x.astype(BF)
            center, inv_two = centered(mid[rows, :].astype(F32))
            n2[rows, :] = (center * inv_two * mg[...] + mb[...]).astype(BF)

    def hidden():
        return hid[...].reshape(quarter * chunk, width)

    def channel_block(h, block):
        cols = pl.ds(pl.multiple_of(block * width, width), width)
        grad = gout[h].reshape(quarter * chunk, width)
        value, back = gelu_parts(dot(n2[...], cu[:, cols]) + cub[:, cols])
        hid[...] = value.astype(BF).reshape(quarter, chunk, width)
        pre = back * dot(grad, cd[cols, :], 1, 1)
        dpre[...] = pre.astype(BF)
        up_bias[:, cols] += jnp.sum(pre, 0, keepdims=True)
        out = dot(hidden(), cd[cols, :])
        for t in range(width // 128):
            stage[t] += out[:, t * 128 : (t + 1) * 128]
        dn_acc[...] += dot(dpre[...], cu[:, cols], 1, 1)
        for g, (left, right) in enumerate(((dpre[...], n2[...]), (hidden(), grad))):
            part = dot(left, right, 0, 0)
            if h > 0:
                part = part + gbuf[g, cols, :].astype(F32)
            gbuf[g, cols, :] = part.astype(BF)

    def finish_rows(h):
        gain_sum = jnp.zeros((SUB, width), F32)
        bias_sum = jnp.zeros((SUB, width), F32)
        valid = valid_of(h)
        for start, count in tiles:
            rows = pl.ds(start * chunk, count * chunk)
            x = mid[rows, :].astype(F32)
            out = jnp.concatenate([stage[t, rows, :] for t in range(width // 128)], 1)
            out = (x + out + cdb[...]).reshape(count, chunk, width) * valid
            hid[start : start + count] = out.astype(BF)
            center, inv_two = centered(x)
            norm_two = center * inv_two
            dn = dn_acc[rows, :]
            gain_sum += jnp.sum((norm_two * dn).reshape(-1, SUB, width), 0)
            bias_sum += jnp.sum(dn.reshape(-1, SUB, width), 0)
            scaled = dn * mg[...]
            one = jnp.sum(scaled, 1, keepdims=True) * (1.0 / width)
            two = jnp.sum(scaled * norm_two, 1, keepdims=True) * (1.0 / width)
            grad = gout[h, start : start + count].reshape(count * chunk, width).astype(F32)
            grad = grad + inv_two * (scaled - one - norm_two * two)
            grad = grad.reshape(count, 2, SUB, width)
            first, second = grad[:, 0], grad[:, 1]
            for k in range(n_mp):
                base = 3 * (k // 2)
                if k % 2 == 0:
                    sides = (tile(first, base), tile(second, base))
                    middle = jnp.where(low_half, tile(first, base + 1), swap(tile(second, base + 1)))
                else:
                    sides = (tile(first, base + 2), tile(second, base + 2))
                    middle = jnp.where(low_half, swap(tile(second, base + 1)), tile(first, base + 1))
                rows_out = jnp.concatenate([sides[0], middle, sides[1]], 2)
                rows_out = rows_out.reshape(count * SUB, 3 * 128)
                if count % 2:
                    rows_out = jnp.concatenate([rows_out, jnp.zeros((SUB, 3 * 128), F32)], 0)
                send[h, k, start * SUB : (start + count + count % 2) * SUB, :] = rows_out.astype(BF)
        frecv[h, me] = send[h, me]
        return jnp.sum(gain_sum, 0, keepdims=True), jnp.sum(bias_sum, 0, keepdims=True)

    def out_copy(h):
        return pltpu.make_async_copy(hid, bo_hbm.at[:, pl.ds(h * chunk, chunk)], out_sem.at[h])

    def put(first_row, vector):
        for i in range(vector.shape[1] // 384):
            small[first_row + i : first_row + i + 1, :] = vector[:, i * 384 : (i + 1) * 384]

    small[400:416, :] = jnp.zeros((16, 384), F32)
    put(412, down_bias)
    loads[1].wait()
    loads[4].wait()
    totals = []

    def run_channel(h):
        for step in range(1, n_mp):
            forward_copy(h, step).wait()
        layer_norm_two(h)
        for step in range(1, n_mp):
            pl.semaphore_signal(
                credit.at[h], 1, device_id={"mp": peer(step)}, device_id_type=pl.DeviceIdType.MESH
            )
        stage[...] = jnp.zeros_like(stage)
        if h > 0:
            out_copy(0).wait()
        dn_acc[...] = jnp.zeros_like(dn_acc)

        @pl.loop(0, blocks)
        def _(block):
            channel_block(h, block)

        totals.append(finish_rows(h))
        pl.semaphore_wait(credit.at[h], n_mp - 1)
        for step in (2, 1, 3):
            backward_copy(h, step).start()
        out_copy(h).start()

    up_bias[...] = jnp.zeros_like(up_bias)
    run_channel(0)
    run_channel(1)
    put(400, up_bias[...])
    put(408, totals[0][0] + totals[1][0])
    put(410, totals[0][1] + totals[1][1])
    grad_out = pltpu.make_async_copy(gbuf, gch_hbm, out_sem.at[2])
    grad_out.start()

    rows = lax.broadcasted_iota(jnp.int32, (HALF, 6 * HALF), 0)
    cols = lax.broadcasted_iota(jnp.int32, (HALF, 6 * HALF), 1)
    perm = jnp.zeros((6 * HALF, 6 * HALF), F32)
    all_rows = lax.broadcasted_iota(jnp.int32, (6 * HALF, 6 * HALF), 0)
    all_cols = lax.broadcasted_iota(jnp.int32, (6 * HALF, 6 * HALF), 1)
    for place in range(6):
        inside = (all_cols >= place * HALF) & (all_cols < (place + 1) * HALF)
        same = all_rows == all_cols + (slot_blocks(place) - place) * HALF
        perm = perm + jnp.where(inside & same, 1.0, 0.0)
    perm = perm.astype(BF)

    acc_g[...] = jnp.zeros_like(acc_g)
    acc_b[...] = jnp.zeros_like(acc_b)
    gtu[...] = jnp.zeros_like(gtu)
    gtd[...] = jnp.zeros_like(gtd)
    stat_out[...] = jnp.zeros_like(stat_out)

    def token_backward(h):
        for step in range(1, n_mp):
            backward_copy(h, step).wait()
        for k in range(n_mp):
            for t in range(3):
                part = frecv[h, k, :qrows, t * 128 : (t + 1) * 128]
                low_row = (k % 2) * qrows
                stage[2 * t + k // 2, low_row : low_row + qrows, :] = part.astype(F32)

        @pl.loop(0, pairs)
        def _(j):
            b = h * chunk + j
            q = h * pairs + j
            slots = [
                jnp.concatenate([stage[2 * t + i, pl.ds(j, half_p, stride=SUB), :] for i in range(2)], 0)
                for t in range(3)
            ]
            slots = jnp.concatenate(slots, 1).astype(BF)
            grad = dot(perm, slots, 1, 1)
            low = grad.astype(BF)
            gtd[...] += dot(slots, slot_rows(mixed_all, q))
            pre = back_all[q].astype(F32) * dot(low, td[...])
            pre_low = pre.astype(BF)
            small[414:415, :] += jnp.sum(pre, 0, keepdims=True)
            small[415:416, :patches] += jnp.sum(grad, 0, keepdims=True)
            norm = jnp.concatenate([norm_of(b + e * pairs) for e in range(2)], 0)
            gains = jnp.concatenate([gain_one, gain_one], 0)
            normed = (norm * gains + jnp.concatenate([bias_one, bias_one], 0)).astype(BF)
            gtu[...] += dot(normed, pre_low, 0, 0)
            dn = dot(pre_low, tu[...], 1, 1)
            prod = norm * dn
            acc_g[...] += prod[:local] + prod[local:]
            acc_b[...] += dn[:local] + dn[local:]
            scaled = dn * gains
            second = prod * gains
            for e in range(2):
                part = slice(e * local, (e + 1) * local)
                stat_out[pl.ds(b + e * pairs, 1), :] = jnp.sum(scaled[part], 0, keepdims=True)
                stat_out[pl.ds(images + b + e * pairs, 1), :] = jnp.sum(second[part], 0, keepdims=True)
            mixed_all[q, :, :patches] = low
            back_all[q, :, :patches] = scaled.astype(BF)

    token_backward(0)
    token_backward(1)
    share_stats(1)
    small[0:patches, :] = gtu[...]
    small[200 : 200 + patches, :] = gtd[...]
    gpre[0] = acc_g[...]
    gpre[1] = acc_b[...]
    wait_stats(1)
    sums = [stat_in[1, k] for k in range(n_mp)]
    stat_out[...] = (sums[0] + sums[1] + sums[2] + sums[3]) * (1.0 / width)

    @pl.loop(0, images // 2)
    def _(q):
        h = q // pairs
        b = h * chunk + q - h * pairs
        for e in range(2):
            image = b + e * pairs
            part = slice(e * local, (e + 1) * local)
            one = stat_out[pl.ds(image, 1), :]
            two = stat_out[pl.ds(images + image, 1), :]
            scaled = back_all[q, part, :patches].astype(F32)
            grad = mixed_all[q, part, :patches].astype(F32)
            grad = grad + mean_inv[1, pl.ds(image, 1), :] * (scaled - one - norm_of(image) * two)
            img[image] = grad.astype(BF)

    image_out = pltpu.make_async_copy(img, gi_hbm, out_sem.at[3])
    image_out.start()
    out_copy(1).wait()
    grad_out.wait()
    image_out.wait()


def shards(
    axes, images, counts, pre_gain, pre_bias, token_up, token_up_bias, token_down, token_down_bias,
    mid_gain, mid_bias, channel_up, channel_up_bias, channel_down, channel_down_bias, cotangent,
):
    n_dp, n_mp = axes
    count, patches, local = images.shape
    width, hidden = channel_up.shape
    units = token_up.shape[1]
    quarter = cotangent.shape[1]
    chunk = count // 2
    rows = quarter * chunk
    qpad = -(-quarter * SUB // 16) * 16
    offset = lax.axis_index("mp") * local
    gain = lax.dynamic_slice_in_dim(pre_gain, offset, local)
    bias = lax.dynamic_slice_in_dim(pre_bias, offset, local)

    def spread(vector):
        return jnp.broadcast_to(vector[:, None], (vector.shape[0], 128))

    any_space = pl.BlockSpec(memory_space=pl.ANY)
    vmem = pl.BlockSpec(memory_space=pltpu.VMEM)
    smem = pl.BlockSpec(memory_space=pltpu.SMEM)
    V = pltpu.VMEM
    dma = pltpu.SemaphoreType.DMA
    out = pl.pallas_call(
        functools.partial(kernel, axes),
        out_shape=(
            jax.ShapeDtypeStruct((quarter, count, width), BF),
            jax.ShapeDtypeStruct((count, local, patches), BF),
            jax.ShapeDtypeStruct((2, hidden, width), BF),
            jax.ShapeDtypeStruct((416, units), F32),
            jax.ShapeDtypeStruct((2, local, patches), F32),
        ),
        in_specs=[smem] + [any_space] * 4 + [vmem] * 10,
        out_specs=(any_space, any_space, any_space, vmem, vmem),
        scratch_shapes=[
            V((count, local, patches), BF),
            V((width, hidden), BF),
            V((hidden, width), BF),
            V((2, quarter, chunk, width), BF),
            V((2 * count, patches), F32),
            V((2, n_mp, 2 * count, patches), F32),
            V((2, count, patches), F32),
            V((count // 2, 2 * local, units), BF),
            V((count // 2, 2 * local, units), BF),
            V((width // 128, rows, 128), F32),
            V((2, n_mp, qpad, 2 * local), BF),
            V((2, n_mp, qpad, 2 * local), BF),
            V((rows, width), BF),
            V((rows, width), BF),
            V((quarter, chunk, width), BF),
            V((rows, width), BF),
            V((rows, width), F32),
            V((2, hidden, width), BF),
            V((local, patches), F32),
            V((local, patches), F32),
            V((patches, units), F32),
            V((patches, units), F32),
            V((1, hidden), F32),
            dma((5,)),
            dma((4,)),
            dma((2, n_mp - 1)),
            dma((2, n_mp - 1)),
            dma((2, n_mp - 1)),
            dma((2, n_mp - 1)),
            dma((2, n_mp - 1)),
            dma((2, n_mp - 1)),
            pltpu.SemaphoreType.REGULAR((2,)),
        ],
        compiler_params=pltpu.CompilerParams(
            collective_id=0, has_side_effects=True, vmem_limit_bytes=64 * 2**20 - 2**17
        ),
    )(
        counts,
        jnp.transpose(images, (0, 2, 1)),
        jnp.transpose(cotangent, (1, 0, 2)),
        channel_up,
        channel_down,
        token_up,
        jnp.transpose(token_down),
        token_up_bias[None],
        spread(token_down_bias),
        spread(gain),
        spread(bias),
        mid_gain[None],
        mid_bias[None],
        channel_up_bias[None],
        channel_down_bias[None],
    )
    block_out, grad_images, grads, small, gpre = out
    both = ("dp", "mp")
    wide = lax.psum_scatter(grads.astype(F32), both, scatter_dimension=1, tiled=True)
    blank = jnp.zeros((2, width), F32)
    gpre = lax.dynamic_update_slice_in_dim(blank, jnp.sum(gpre, 2), offset, 1)
    small, gpre = lax.psum((small, gpre), both)
    return (
        jnp.transpose(block_out, (1, 0, 2)),
        jnp.transpose(grad_images, (0, 2, 1)),
        gpre[0],
        gpre[1],
        small[:patches],
        small[414],
        jnp.transpose(small[200 : 200 + patches]),
        small[415, :patches],
        small[408:410].reshape(width),
        small[410:412].reshape(width),
        jnp.transpose(wide[0]),
        small[400:408].reshape(hidden),
        wide[1],
        small[412:414].reshape(width),
    )


def solution(mesh):
    axes = (mesh.shape["dp"], mesh.shape["mp"])
    in_specs = (P("dp", None, "mp"), P("dp")) + (P(),) * 12 + (P("dp", "mp", None),)
    out_specs = (
        (P("dp", "mp", None), P("dp", None, "mp"))
        + (P(),) * 8
        + (P(None, ("dp", "mp")), P(), P(("dp", "mp"), None), P())
    )
    return jax.shard_map(
        functools.partial(shards, axes), mesh=mesh, in_specs=in_specs, out_specs=out_specs, check_vma=False
    )
```

```python
import functools

import jax
import jax.numpy as jnp
from jax import lax
from jax.experimental import pallas as pl
from jax.experimental.pallas import tpu as pltpu
from jax.sharding import PartitionSpec as P

EPSILON = 1e-06
GELU_ROOT = 0.7978845608028654
GELU_CUBE = 0.044715
BF = jnp.bfloat16
F32 = jnp.float32
HALF = 64
SUB = 8


def dot(left, right, left_dim=1, right_dim=0):
    return lax.dot_general(
        left, right, (((left_dim,), (right_dim,)), ((), ())), preferred_element_type=F32
    )


def gelu(x):
    half = 0.5 * x
    return half + half * jnp.tanh(x * (x * x * (GELU_ROOT * GELU_CUBE) + GELU_ROOT))


def gelu_parts(x):
    squares = x * x
    slope = squares * (GELU_ROOT * GELU_CUBE) + GELU_ROOT
    t = jnp.tanh(x * slope)
    half = 0.5 * x
    value = half + half * t
    inner = slope + squares * (2.0 * GELU_ROOT * GELU_CUBE)
    back = (0.5 + 0.5 * t) + (half * inner) * (1.0 - t * t)
    return value, back


def kernel(axes, fused, *refs):
    (
        counts, img_hbm, cot_hbm, cu_hbm, cd_hbm, tu, td, pre_gain, pre_bias, tub, tdb, mg, mb, cub, cdb,
    ) = refs[:15]
    refs = refs[15:]
    bo_hbm, gi_hbm = refs[:2]
    if fused:
        (
            pg_out, pb_out, tu_out, tub_out, td_out, tdb_out, mg_out, mb_out, cu_out, cub_out, cd_out, cdb_out,
        ) = refs[2:14]
        refs = refs[14:]
    else:
        gch_hbm, small_out = refs[2:4]
        refs = refs[4:]
    (
        img, cu, cd, base, stat_out, stat_in, mean_inv, mixed, keep, stage, send, frecv,
        mid, act, dn_acc, gbuf, acc_g, acc_b, up_bias, small, gain_col, bias_col,
        load_sem, out_sem, stat_send, stat_recv, f_send, f_recv, b_send, b_recv, credit,
    ) = refs[:31]
    if fused:
        (
            c_in, xu_in, yd_in, xd_in, zu_in, zd_in, yu_in, y_out, part_out, part_in, whole_in,
            c_sem, x_sem, y_sem, x2_sem, zu_sem, zd_sem, y2_sem, part_sem, whole_sem, core_credit,
        ) = refs[31:]
    n_dp, n_mp = axes
    me = lax.axis_index("mp")
    images, local, patches = img.shape
    chunk = images // 2
    pairs = chunk // 2
    width = n_mp * local
    quarter = patches // n_mp
    qrows = quarter * SUB
    half_p = patches // 2
    blocks = cu.shape[1] // width
    odd = lax.rem(me, 2)

    def peer(step):
        return lax.rem(me + step, n_mp)

    barrier = pltpu.get_barrier_semaphore()
    if fused:
        dp = lax.axis_index("dp")
        devices = n_dp * n_mp
        mine = dp * n_mp + me
        peers = devices - 1

        def device(number):
            return {"dp": number // n_mp, "mp": lax.rem(number, n_mp)}

        @pl.loop(1, devices)
        def _(step):
            other = lax.rem(mine + step, devices)
            pl.semaphore_signal(barrier, 1, device_id=device(other), device_id_type=pl.DeviceIdType.MESH)
    else:
        peers = n_mp - 1
        for step in range(1, n_mp):
            pl.semaphore_signal(barrier, 1, device_id={"mp": peer(step)}, device_id_type=pl.DeviceIdType.MESH)

    loads = [
        pltpu.make_async_copy(img_hbm, img, load_sem.at[0]),
        pltpu.make_async_copy(cd_hbm, cd, load_sem.at[1]),
        pltpu.make_async_copy(cot_hbm.at[:, pl.ds(0, chunk)], base.at[1], load_sem.at[2]),
        pltpu.make_async_copy(cot_hbm.at[:, pl.ds(chunk, chunk)], base.at[2], load_sem.at[3]),
        pltpu.make_async_copy(cu_hbm, cu, load_sem.at[4]),
    ]
    for load in loads:
        load.start()

    loads[0].wait()

    @pl.loop(0, images)
    def _(b):
        x = img[b].astype(F32)
        total = jnp.sum(x, 0, keepdims=True)
        center = x - total * (1.0 / local)
        stat_out[pl.ds(b, 1), :] = total
        stat_out[pl.ds(images + b, 1), :] = jnp.sum(center * center, 0, keepdims=True)

    def stat_copy(phase, step):
        return pltpu.make_async_remote_copy(
            src_ref=stat_out, dst_ref=stat_in.at[phase, me],
            send_sem=stat_send.at[phase, step - 1], recv_sem=stat_recv.at[phase, step - 1],
            device_id={"mp": peer(step)}, device_id_type=pl.DeviceIdType.MESH,
        )

    def share_stats(phase):
        stat_in[phase, me] = stat_out[...]
        for step in (2, 1, 3):
            stat_copy(phase, step).start()

    def wait_stats(phase):
        for step in range(1, n_mp):
            stat_copy(phase, step).wait()

    pl.semaphore_wait(barrier, peers)
    share_stats(0)

    row = lax.broadcasted_iota(jnp.int32, (chunk, width), 0)
    for load in loads[2:4]:
        load.wait()

    def valid_of(h):
        return jnp.where(row + h * chunk < counts[0], 1.0, 0.0)[None]

    down_bias = jnp.zeros((chunk, width), F32)
    for h in range(2):
        masked = base[1 + h].astype(F32) * valid_of(h)
        base[1 + h] = masked.astype(BF)
        down_bias = down_bias + jnp.sum(masked, 0)
    down_bias = jnp.sum(down_bias, 0, keepdims=True)

    wait_stats(0)
    sums = [stat_in[0, k] for k in range(n_mp)]
    mean = sum(s[:images] for s in sums) * (1.0 / width)
    square = sum(s[images:] for s in sums)
    for s in sums:
        gap = s[:images] * (1.0 / local) - mean
        square = square + float(local) * (gap * gap)
    mean_inv[0] = mean
    mean_inv[1] = lax.rsqrt(square * (1.0 / width) + EPSILON)

    eye = jnp.where(
        lax.broadcasted_iota(jnp.int32, (patches, patches), 0)
        == lax.broadcasted_iota(jnp.int32, (patches, patches), 1), 1.0, 0.0,
    ).astype(BF)

    def line(ref):
        return ref[...].reshape(1, ref.shape[0])

    def columns(row):
        return jnp.transpose(jnp.broadcast_to(row, (128, 128)))

    for ref, col in ((pre_gain, gain_col), (pre_bias, bias_col)):
        values = line(ref)
        for i in range(width // 128):
            dn_acc[i * 128 : (i + 1) * 128, :128] = columns(values[:, i * 128 : (i + 1) * 128])
        start = pl.multiple_of(me * local, HALF)
        col[...] = dn_acc[pl.ds(start, local), :128]

    def lanes(ref):
        tile = ref[...]
        return jnp.concatenate([tile, tile], 1)[:, :patches]

    gain_one, bias_one = lanes(gain_col), lanes(bias_col)
    values = line(tdb)
    values = jnp.concatenate([values, jnp.zeros((1, 256 - patches), F32)], 1)
    column = jnp.concatenate([columns(values[:, :128]), columns(values[:, 128:])], 0)[:patches]
    token_down_bias = jnp.concatenate([column] * 3, 1)
    token_up_bias, mid_gain, mid_bias, down_bias_row = line(tub), line(mg), line(mb), line(cdb)

    def norm_of(b):
        return (img[b].astype(F32) - mean_inv[0, pl.ds(b, 1), :]) * mean_inv[1, pl.ds(b, 1), :]

    def slot_blocks(place):
        even = (0, 1, 2, 5, 3, 4)[place]
        other = (1, 2, 3, 0, 4, 5)[place]
        return even + odd * (other - even)

    def slot_rows(ref, q):
        rows = []
        for place in range(6):
            start = pl.multiple_of(slot_blocks(place) * HALF, HALF)
            rows.append(ref[q, pl.ds(start, HALF), :])
        return jnp.concatenate(rows, 0)

    def slot_images(b):
        rows = []
        for place in range(6):
            block = slot_blocks(place)
            which = block // 3
            start = pl.multiple_of((block - 3 * which) * HALF, HALF)
            rows.append(img[b + pairs * which, pl.ds(start, HALF), :])
        return jnp.concatenate(rows, 0)

    def forward_copy(h, step):
        return pltpu.make_async_remote_copy(
            src_ref=send.at[h, peer(step)], dst_ref=frecv.at[h, me],
            send_sem=f_send.at[h, step - 1], recv_sem=f_recv.at[h, step - 1],
            device_id={"mp": peer(step)}, device_id_type=pl.DeviceIdType.MESH,
        )

    def backward_copy(h, step):
        return pltpu.make_async_remote_copy(
            src_ref=send.at[h, peer(step)], dst_ref=frecv.at[h, me],
            send_sem=b_send.at[h, step - 1], recv_sem=b_recv.at[h, step - 1],
            device_id={"mp": peer(step)}, device_id_type=pl.DeviceIdType.MESH,
        )

    def token_forward(h):
        @pl.loop(0, pairs)
        def _(j):
            b = h * chunk + j
            q = lax.rem(j, 2)
            normed = jnp.concatenate(
                [(norm_of(b + e * pairs) * gain_one + bias_one).astype(BF) for e in range(2)], 0
            )
            mixed[q] = gelu(dot(normed, tu[...]) + token_up_bias).astype(BF)
            out = dot(td[...], slot_rows(mixed, q), 1, 1)
            out = out + dot(eye, slot_images(b), 1, 1) + token_down_bias
            for t in range(3):
                for side in range(2):
                    part = out[side * half_p : (side + 1) * half_p, t * 128 : (t + 1) * 128]
                    stage[2 * t + side, pl.ds(j, half_p, stride=SUB), :] = part

        for k in range(n_mp):
            for t in range(3):
                low_row = (k % 2) * qrows
                part = stage[2 * t + k // 2, low_row : low_row + qrows, :]
                send[h, k, :qrows, t * 128 : (t + 1) * 128] = part.astype(BF)
        frecv[h, me] = send[h, me]
        for step in (2, 1, 3):
            forward_copy(h, step).start()

    token_forward(0)
    token_forward(1)

    low_half = lax.broadcasted_iota(jnp.int32, (1, 1, 128), 2) < HALF
    tiles = [(12 * i, 12) for i in range(quarter // 12)]
    tiles += [(12 * (quarter // 12), quarter % 12)] if quarter % 12 else []

    def arrived(ref, h, k, start, count):
        padded = count + count % 2
        rows = ref[h, k, start * SUB : (start + padded) * SUB, :].astype(F32)
        return rows[: count * SUB].reshape(count, SUB, 3 * 128)

    def tile(array, i):
        return array[:, :, i * 128 : (i + 1) * 128]

    def swap(array):
        count = array.shape[0]
        return pltpu.roll(array.reshape(count * SUB, 128), HALF, 1).reshape(count, SUB, 128)

    def merge(h, start, count):
        parts = [arrived(frecv, h, k, start, count) for k in range(n_mp)]
        first, second = [], []
        for k in range(0, n_mp, 2):
            a, b = parts[k], parts[k + 1]
            first += [tile(a, 0), jnp.where(low_half, tile(a, 1), tile(b, 1)), tile(b, 0)]
            second += [tile(a, 2), swap(jnp.where(low_half, tile(b, 1), tile(a, 1))), tile(b, 2)]
        rows = jnp.stack([jnp.concatenate(first, 2), jnp.concatenate(second, 2)], 1)
        return rows.reshape(count * 2 * SUB, width)

    def centered(x):
        center = x - jnp.sum(x, 1, keepdims=True) * (1.0 / width)
        spread_two = jnp.sum(center * center, 1, keepdims=True) * (1.0 / width)
        return center, lax.rsqrt(spread_two + EPSILON)

    def layer_norm_two(h):
        for start, count in tiles:
            rows = pl.ds(start * chunk, count * chunk)
            x = merge(h, start, count)
            mid[rows, :] = x.astype(BF)
            center, inv_two = centered(mid[rows, :].astype(F32))
            normed = (center * inv_two * mid_gain + mid_bias).astype(BF)
            base[0, start : start + count] = normed.reshape(count, chunk, width)

    def flat(ref, i):
        return ref[i].reshape(quarter * chunk, width)

    def channel_block(h, block):
        cols = pl.ds(pl.multiple_of(block * width, width), width)
        grad = dot(flat(base, 1 + h), cd[cols, :], 1, 1)
        act[0] = grad.astype(BF).reshape(quarter, chunk, width)
        value, back = gelu_parts(dot(flat(base, 0), cu[:, cols]) + cub[cols].reshape(1, width))
        act[1] = value.astype(BF).reshape(quarter, chunk, width)
        pre = back * flat(act, 0).astype(F32)
        act[0] = pre.astype(BF).reshape(quarter, chunk, width)
        up_bias[:, cols] += jnp.sum(pre, 0, keepdims=True)
        out = dot(flat(act, 1), cd[cols, :])
        for t in range(width // 128):
            stage[t] += out[:, t * 128 : (t + 1) * 128]
        dn_acc[...] += dot(flat(act, 0), cu[:, cols], 1, 1)

        @pl.loop(0, 2)
        def _(g):
            part = dot(flat(act, g), flat(base, g * (1 + h)), 0, 0).reshape(gbuf.shape[2:])
            if h > 0:
                part = part + gbuf[g, block].astype(F32)
            gbuf[g, block] = part.astype(BF)

    def finish_rows(h):
        gain_sum = jnp.zeros((SUB, width), F32)
        bias_sum = jnp.zeros((SUB, width), F32)
        valid = valid_of(h)
        for start, count in tiles:
            rows = pl.ds(start * chunk, count * chunk)
            x = mid[rows, :].astype(F32)
            out = jnp.concatenate([stage[t, rows, :] for t in range(width // 128)], 1)
            out = (x + out + down_bias_row).reshape(count, chunk, width) * valid
            act[1, start : start + count] = out.astype(BF)
            center, inv_two = centered(x)
            norm_two = center * inv_two
            dn = dn_acc[rows, :]
            gain_sum += jnp.sum((norm_two * dn).reshape(-1, SUB, width), 0)
            bias_sum += jnp.sum(dn.reshape(-1, SUB, width), 0)
            scaled = dn * mid_gain
            one = jnp.sum(scaled, 1, keepdims=True) * (1.0 / width)
            two = jnp.sum(scaled * norm_two, 1, keepdims=True) * (1.0 / width)
            grad = base[1 + h, start : start + count].reshape(count * chunk, width).astype(F32)
            grad = grad + inv_two * (scaled - one - norm_two * two)
            grad = grad.reshape(count, 2, SUB, width)
            first, second = grad[:, 0], grad[:, 1]
            for k in range(n_mp):
                left = 3 * (k // 2)
                if k % 2 == 0:
                    sides = (tile(first, left), tile(second, left))
                    middle = jnp.where(low_half, tile(first, left + 1), swap(tile(second, left + 1)))
                else:
                    sides = (tile(first, left + 2), tile(second, left + 2))
                    middle = jnp.where(low_half, swap(tile(second, left + 1)), tile(first, left + 1))
                rows_out = jnp.concatenate([sides[0], middle, sides[1]], 2)
                rows_out = rows_out.reshape(count * SUB, 3 * 128)
                if count % 2:
                    rows_out = jnp.concatenate([rows_out, jnp.zeros((SUB, 3 * 128), F32)], 0)
                send[h, k, start * SUB : (start + count + count % 2) * SUB, :] = rows_out.astype(BF)
        frecv[h, me] = send[h, me]
        return jnp.sum(gain_sum, 0, keepdims=True), jnp.sum(bias_sum, 0, keepdims=True)

    if fused:
        z, x = dp // 2, lax.rem(dp, 2)
        y, c = me // 2, odd

        def at(zz, xx, yy, cc):
            return {"dp": zz * 2 + xx, "mp": yy * 2 + cc}

        def block_at(t):
            return lax.rem(z + 1 + t, blocks)

        def remote(src, dst, sems, index, target):
            return pltpu.make_async_remote_copy(
                src_ref=src, dst_ref=dst, send_sem=sems.at[0, index], recv_sem=sems.at[1, index],
                device_id=target, device_id_type=pl.DeviceIdType.MESH,
            )

        def core_copy(t):
            return remote(gbuf.at[:, block_at(t), :, :, 1 - c], c_in, c_sem, 0, at(z, x, y, 1 - c))

        def xu_copy(t):
            return remote(gbuf.at[0, block_at(t), 1 - x, :, c], xu_in.at[t], x_sem, t, at(z, 1 - x, y, c))

        def yd_copy(t):
            return remote(gbuf.at[1, block_at(t), :, 1 - y, c], yd_in.at[t], y_sem, t, at(z, x, 1 - y, c))

        def xd_copy(t):
            return remote(gbuf.at[1, block_at(t), 1 - x, y, c], xd_in.at[t], x2_sem, t, at(z, 1 - x, y, c))

        def zu_copy(t):
            return remote(gbuf.at[0, block_at(t), x, :, c], zu_in.at[t], zu_sem, t, at(block_at(t), x, y, c))

        def zd_copy(t):
            return remote(gbuf.at[1, block_at(t), x, y, c], zd_in.at[t], zd_sem, t, at(block_at(t), x, y, c))

        def add(ref, part):
            ref[...] = (ref[...].astype(F32) + part.astype(F32)).astype(BF)

        def end_core(t):
            core_copy(t).wait()
            for g in range(2):
                for xx in range(2):
                    for yy in range(2):
                        add(gbuf.at[g, block_at(t), xx, yy, c], c_in[g, xx, yy])

        def start_first(t):
            xu_copy(t).start()
            yd_copy(t).start()

        def end_first(t):
            xu_copy(t).wait()
            yd_copy(t).wait()
            for i in range(2):
                add(gbuf.at[0, block_at(t), x, i, c], xu_in[t, i])
                add(gbuf.at[1, block_at(t), i, y, c], yd_in[t, i])

        def end_second(t):
            xd_copy(t).wait()
            add(gbuf.at[1, block_at(t), x, y, c], xd_in[t])

        def scatter_step(t):
            @pl.when(t >= 1)
            def _():
                end_core(t - 1)
                start_first(t - 1)
                pl.semaphore_signal(
                    core_credit, 1, device_id=at(z, x, y, 1 - c), device_id_type=pl.DeviceIdType.MESH
                )
                pl.semaphore_wait(core_credit, 1)

            core_copy(t).start()

            @pl.when(t >= 2)
            def _():
                end_first(t - 2)
                zu_copy(t - 2).start()
                xd_copy(t - 2).start()

            @pl.when(t >= 3)
            def _():
                end_second(t - 3)
                zd_copy(t - 3).start()

    def out_copy(h):
        return pltpu.make_async_copy(act.at[1], bo_hbm.at[:, pl.ds(h * chunk, chunk)], out_sem.at[h])

    def put(first_row, vector):
        for i in range(vector.shape[1] // 384):
            small[first_row + i : first_row + i + 1, :] = vector[:, i * 384 : (i + 1) * 384]

    small[...] = jnp.zeros_like(small)
    put(412, down_bias)
    loads[1].wait()
    loads[4].wait()
    totals = []

    def run_channel(h):
        for step in range(1, n_mp):
            forward_copy(h, step).wait()
        layer_norm_two(h)
        for step in range(1, n_mp):
            pl.semaphore_signal(
                credit.at[h], 1, device_id={"mp": peer(step)}, device_id_type=pl.DeviceIdType.MESH
            )
        stage[...] = jnp.zeros_like(stage)
        if h > 0:
            out_copy(0).wait()
        dn_acc[...] = jnp.zeros_like(dn_acc)

        @pl.loop(0, blocks)
        def _(t):
            block = block_at(t) if fused else t
            channel_block(h, block)
            if fused and h > 0:
                scatter_step(t)

        totals.append(finish_rows(h))
        pl.semaphore_wait(credit.at[h], n_mp - 1)
        for step in (2, 1, 3):
            backward_copy(h, step).start()
        out_copy(h).start()

    up_bias[...] = jnp.zeros_like(up_bias)
    run_channel(0)
    run_channel(1)
    put(400, up_bias[...])
    put(408, totals[0][0] + totals[1][0])
    put(410, totals[0][1] + totals[1][1])
    last = blocks - 1
    if fused:
        end_core(last)
        start_first(last)
        end_first(last - 1)
        zu_copy(last - 1).start()
        xd_copy(last - 1).start()
        end_second(last - 2)
        zd_copy(last - 2).start()
    else:
        grad_out = pltpu.make_async_copy(gbuf, gch_hbm, out_sem.at[2])
        grad_out.start()

    rows = lax.broadcasted_iota(jnp.int32, (HALF, 6 * HALF), 0)
    cols = lax.broadcasted_iota(jnp.int32, (HALF, 6 * HALF), 1)
    perm = jnp.zeros((6 * HALF, 6 * HALF), F32)
    all_rows = lax.broadcasted_iota(jnp.int32, (6 * HALF, 6 * HALF), 0)
    all_cols = lax.broadcasted_iota(jnp.int32, (6 * HALF, 6 * HALF), 1)
    for place in range(6):
        inside = (all_cols >= place * HALF) & (all_cols < (place + 1) * HALF)
        same = all_rows == all_cols + (slot_blocks(place) - place) * HALF
        perm = perm + jnp.where(inside & same, 1.0, 0.0)
    perm = perm.astype(BF)

    acc_g[...] = jnp.zeros_like(acc_g)
    acc_b[...] = jnp.zeros_like(acc_b)
    stat_out[...] = jnp.zeros_like(stat_out)

    def token_backward(h):
        for step in range(1, n_mp):
            backward_copy(h, step).wait()
        for k in range(n_mp):
            for t in range(3):
                part = frecv[h, k, :qrows, t * 128 : (t + 1) * 128]
                low_row = (k % 2) * qrows
                stage[2 * t + k // 2, low_row : low_row + qrows, :] = part.astype(F32)

        @pl.loop(0, pairs)
        def _(j):
            b = h * chunk + j
            q = lax.rem(j, 2)
            slots = [
                jnp.concatenate([stage[2 * t + i, pl.ds(j, half_p, stride=SUB), :] for i in range(2)], 0)
                for t in range(3)
            ]
            slots = jnp.concatenate(slots, 1).astype(BF)
            grad = dot(perm, slots, 1, 1)
            low = grad.astype(BF)
            norm = jnp.concatenate([norm_of(b + e * pairs) for e in range(2)], 0)
            gains = jnp.concatenate([gain_one, gain_one], 0)
            normed = (norm * gains + jnp.concatenate([bias_one, bias_one], 0)).astype(BF)
            value, back = gelu_parts(dot(normed, tu[...]) + token_up_bias)
            mixed[q] = value.astype(BF)
            small[200 : 200 + patches, :] += dot(slots, slot_rows(mixed, q))
            pre = back * dot(low, td[...])
            pre_low = pre.astype(BF)
            small[414:415, :] += jnp.sum(pre, 0, keepdims=True)
            small[415:416, :patches] += jnp.sum(grad, 0, keepdims=True)
            small[:patches, :] += dot(normed, pre_low, 0, 0)
            dn = dot(pre_low, tu[...], 1, 1)
            prod = norm * dn
            acc_g[...] += prod[:local] + prod[local:]
            acc_b[...] += dn[:local] + dn[local:]
            scaled = dn * gains
            second = prod * gains
            for e in range(2):
                part = slice(e * local, (e + 1) * local)
                stat_out[pl.ds(b + e * pairs, 1), :] = jnp.sum(scaled[part], 0, keepdims=True)
                stat_out[pl.ds(images + b + e * pairs, 1), :] = jnp.sum(second[part], 0, keepdims=True)
                kept = grad[part] + mean_inv[1, pl.ds(b + e * pairs, 1), :] * scaled[part]
                keep[b + e * pairs] = kept.astype(BF)

    token_backward(0)
    if fused:
        end_first(last)
        xd_copy(last).start()
        end_second(last - 1)
        zd_copy(last - 1).start()
    token_backward(1)
    share_stats(1)
    for first, acc in ((416, acc_g), (418, acc_b)):
        column = jnp.broadcast_to(jnp.sum(acc[...], 1, keepdims=True), (local, 128))
        column = jnp.concatenate([column, jnp.zeros((256 - local, 128), F32)], 0)
        values = jnp.concatenate([jnp.transpose(column)[:SUB], jnp.zeros((SUB, 128), F32)], 1)
        values = jnp.where(odd > 0, pltpu.roll(values, local, 1), values)[:1]
        for i in range(n_mp // 2):
            small[first + i : first + i + 1, :] = jnp.where(me // 2 == i, values, 0.0)
    if fused:
        part_out[...] = small[...].astype(BF).reshape(part_out.shape)

        def part_copy(step):
            other = lax.rem(mine + step, devices)
            return remote(part_out.at[other], part_in.at[step], part_sem, step, device(other))

        def whole_copy(step):
            other = lax.rem(mine + step, devices)
            return remote(part_out.at[mine], whole_in.at[mine], whole_sem, step, device(other))

        @pl.loop(1, devices)
        def _(step):
            part_copy(step).start()

        end_second(last)
        for step in range(last):
            zu_copy(step).wait()
        gu = [gbuf[0, z, x, i, c].astype(F32) for i in range(2)]
        for step in range(last):
            gu = [gu[i] + zu_in[step, i].astype(F32) for i in range(2)]
        y_out[...] = jnp.where(y > 0, gu[0], gu[1]).astype(BF)
        last_copy = remote(y_out, yu_in, y2_sem, 0, at(z, x, 1 - y, c))
        last_copy.start()
        cu_out[...] = jnp.where(y > 0, gu[1], gu[0])
        for step in range(last):
            zd_copy(step).wait()
        gd = gbuf[1, z, x, y, c].astype(F32)
        for step in range(last):
            gd = gd + zd_in[step].astype(F32)
        cd_out[...] = gd

    wait_stats(1)
    sums = [stat_in[1, k] for k in range(n_mp)]
    stat_out[...] = (sums[0] + sums[1] + sums[2] + sums[3]) * (1.0 / width)

    @pl.loop(0, images)
    def _(b):
        one = stat_out[pl.ds(b, 1), :]
        two = stat_out[pl.ds(images + b, 1), :]
        grad = keep[b].astype(F32) - mean_inv[1, pl.ds(b, 1), :] * (one + norm_of(b) * two)
        keep[b] = grad.astype(BF)

    image_out = pltpu.make_async_copy(keep, gi_hbm, out_sem.at[3])
    image_out.start()
    if fused:
        @pl.loop(1, devices)
        def _(step):
            part_copy(step).wait()

        total = part_out[mine].astype(F32)
        for step in range(1, devices):
            total = total + part_in[step].astype(F32)
        part_out[mine] = total.astype(BF)

        @pl.loop(1, devices)
        def _(step):
            whole_copy(step).start()

        whole_in[mine] = part_out[mine]
        last_copy.wait()
        cu_out[...] += yu_in[...].astype(F32)

        @pl.loop(1, devices)
        def _(step):
            whole_copy(step).wait()

        small[...] = whole_in[...].astype(F32).reshape(small.shape)
        tu_out[...] = small[:patches, :]
        td_out[...] = small[200 : 200 + patches, :]

        def take(ref, first):
            count = ref.shape[0] // 384
            values = [small[first + i : first + i + 1, :] for i in range(count)]
            ref[...] = jnp.concatenate(values, 1).reshape(ref.shape)

        take(cub_out, 400)
        take(mg_out, 408)
        take(mb_out, 410)
        take(cdb_out, 412)
        take(tub_out, 414)
        tdb_out[...] = small[415:416, :patches].reshape(tdb_out.shape)
        take(pg_out, 416)
        take(pb_out, 418)
    else:
        small_out[...] = small[...]
        grad_out.wait()
    out_copy(1).wait()
    image_out.wait()


def shards(
    axes, images, counts, pre_gain, pre_bias, token_up, token_up_bias, token_down, token_down_bias,
    mid_gain, mid_bias, channel_up, channel_up_bias, channel_down, channel_down_bias, cotangent,
):
    n_dp, n_mp = axes
    count, patches, local = images.shape
    width, hidden = channel_up.shape
    units = token_up.shape[1]
    quarter = cotangent.shape[1]
    chunk = count // 2
    rows = quarter * chunk
    qpad = -(-quarter * SUB // 16) * 16
    fused = n_dp == 8 and n_mp == 4 and hidden == 4 * width
    unit = hidden // 32
    vector = [jax.ShapeDtypeStruct((n,), F32) for n in (width, hidden, units, patches)]
    table = jax.ShapeDtypeStruct((patches, units), F32)
    any_space = pl.BlockSpec(memory_space=pl.ANY)
    vmem = pl.BlockSpec(memory_space=pltpu.VMEM)
    smem = pl.BlockSpec(memory_space=pltpu.SMEM)
    V = pltpu.VMEM
    dma = pltpu.SemaphoreType.DMA
    if fused:
        slab = jax.ShapeDtypeStruct((unit, width), F32)
        grads = (vector[0], vector[0], table, vector[2], table, vector[3]) + (vector[0],) * 2
        grads += (slab, vector[1], slab, vector[0])
        grad_specs = (vmem,) * 12
    else:
        grads = (
            jax.ShapeDtypeStruct((2, hidden // width, 2, 2, 2, unit, width), BF),
            jax.ShapeDtypeStruct((512, units), F32),
        )
        grad_specs = (any_space, vmem)
    pair = dma((2, n_mp - 1))
    extra = [
        V((2, 2, 2, unit, width), BF),
        V((4, 2, unit, width), BF),
        V((4, 2, unit, width), BF),
        V((4, unit, width), BF),
        V((3, 2, unit, width), BF),
        V((3, unit, width), BF),
        V((unit, width), BF),
        V((unit, width), BF),
        V((32, 16, units), BF),
        V((32, 16, units), BF),
        V((32, 16, units), BF),
        dma((2, 1)),
        dma((2, 4)),
        dma((2, 4)),
        dma((2, 4)),
        dma((2, 3)),
        dma((2, 3)),
        dma((2, 1)),
        dma((2, 32)),
        dma((2, 32)),
        pltpu.SemaphoreType.REGULAR,
    ]
    out = pl.pallas_call(
        functools.partial(kernel, axes, fused),
        out_shape=(
            jax.ShapeDtypeStruct((quarter, count, width), BF),
            jax.ShapeDtypeStruct((count, local, patches), BF),
        )
        + grads,
        in_specs=[smem] + [any_space] * 4 + [vmem] * 10,
        out_specs=(any_space, any_space) + grad_specs,
        scratch_shapes=[
            V((count, local, patches), BF),
            V((width, hidden), BF),
            V((hidden, width), BF),
            V((3, quarter, chunk, width), BF),
            V((2 * count, patches), F32),
            V((2, n_mp, 2 * count, patches), F32),
            V((2, count, patches), F32),
            V((2, 2 * local, units), BF),
            V((count, local, patches), BF),
            V((width // 128, rows, 128), F32),
            V((2, n_mp, qpad, 2 * local), BF),
            V((2, n_mp, qpad, 2 * local), BF),
            V((rows, width), BF),
            V((2, quarter, chunk, width), BF),
            V((rows, width), F32),
            V((2, hidden // width, 2, 2, 2, unit, width), BF),
            V((local, patches), F32),
            V((local, patches), F32),
            V((1, hidden), F32),
            V((512, units), F32),
            V((local, 128), F32),
            V((local, 128), F32),
            dma((5,)),
            dma((4,)),
            pair,
            pair,
            pair,
            pair,
            pair,
            pair,
            pltpu.SemaphoreType.REGULAR((2,)),
        ]
        + (extra if fused else []),
        compiler_params=pltpu.CompilerParams(
            collective_id=0, has_side_effects=True, vmem_limit_bytes=64 * 2**20 - 2**17
        ),
    )(
        counts,
        jnp.transpose(images, (0, 2, 1)),
        jnp.transpose(cotangent, (1, 0, 2)),
        channel_up,
        channel_down,
        token_up,
        jnp.transpose(token_down),
        pre_gain,
        pre_bias,
        token_up_bias,
        token_down_bias,
        mid_gain,
        mid_bias,
        channel_up_bias,
        channel_down_bias,
    )
    block_out, grad_images = jnp.transpose(out[0], (1, 0, 2)), jnp.transpose(out[1], (0, 2, 1))
    if fused:
        rest = list(out[2:])
        rest[4] = jnp.transpose(rest[4])
        rest[8] = jnp.transpose(rest[8])
        return (block_out, grad_images, *rest)
    both = ("dp", "mp")
    grads = out[2].reshape(2, hidden, width).astype(F32)
    wide = lax.psum_scatter(grads, both, scatter_dimension=1, tiled=True)
    small = lax.psum(out[3], both)
    return (
        block_out,
        grad_images,
        small[416:418].reshape(width),
        small[418:420].reshape(width),
        small[:patches],
        small[414],
        jnp.transpose(small[200 : 200 + patches]),
        small[415, :patches],
        small[408:410].reshape(width),
        small[410:412].reshape(width),
        jnp.transpose(wide[0]),
        small[400:408].reshape(hidden),
        wide[1],
        small[412:414].reshape(width),
    )


def solution(mesh):
    axes = (mesh.shape["dp"], mesh.shape["mp"])
    in_specs = (P("dp", None, "mp"), P("dp")) + (P(),) * 12 + (P("dp", "mp", None),)
    out_specs = (
        (P("dp", "mp", None), P("dp", None, "mp"))
        + (P(),) * 8
        + (P(None, ("dp", "mp")), P(), P(("dp", "mp"), None), P())
    )
    return jax.shard_map(
        functools.partial(shards, axes), mesh=mesh, in_specs=in_specs, out_specs=out_specs, check_vma=False
    )
```

```python
import functools

import jax
import jax.numpy as jnp
from jax import lax
from jax.experimental import pallas as pl
from jax.experimental.pallas import tpu as pltpu
from jax.sharding import PartitionSpec as P

EPSILON = 1e-06
GELU_ROOT = 0.7978845608028654
GELU_CUBE = 0.044715
BF = jnp.bfloat16
F32 = jnp.float32
HALF = 64
SUB = 8
PARTS = 7
PARTS_EARLY = 27
Y_FIRST = 4
GROUP = 2


def dot(left, right, left_dim=1, right_dim=0):
    return lax.dot_general(
        left, right, (((left_dim,), (right_dim,)), ((), ())), preferred_element_type=F32
    )


def gelu(x):
    half = 0.5 * x
    return half + half * jnp.tanh(x * (x * x * (GELU_ROOT * GELU_CUBE) + GELU_ROOT))


def gelu_parts(x):
    squares = x * x
    slope = squares * (GELU_ROOT * GELU_CUBE) + GELU_ROOT
    t = jnp.tanh(x * slope)
    half = 0.5 * x
    value = half + half * t
    inner = slope + squares * (2.0 * GELU_ROOT * GELU_CUBE)
    back = (0.5 + 0.5 * t) + (half * inner) * (1.0 - t * t)
    return value, back


def kernel(axes, fused, *refs):
    (
        counts, img_hbm, cot_hbm, cu_hbm, cd_hbm, tu, td, pre_gain, pre_bias, tub, tdb, mg, mb, cub, cdb,
    ) = refs[:15]
    refs = refs[15:]
    bo_hbm, gi_hbm = refs[:2]
    if fused:
        sums_out, cu_out, cd_out = refs[2:5]
        refs = refs[5:]
    else:
        gch_hbm, small_out = refs[2:4]
        refs = refs[4:]
    (
        img, cu, cd, base, dh, dh_rest, stat_out, stat_in, mean_inv, mixed, stage, send, frecv,
        mid, act, dn_acc, gbuf, acc_g, acc_b, up_bias, small, gain_col, bias_col,
        load_sem, out_sem, stat_send, stat_recv, f_send, f_recv, b_send, b_recv, credit,
    ) = refs[:32]
    if fused:
        (
            c_in, xu_in, yd_in, xd_in, zu_in, zd_in, yu_in, y_out, part_out, part_in, whole_in,
            c_sem, x_sem, y_sem, x2_sem, zu_sem, zd_sem, y2_sem, part_sem, whole_sem, core_credit,
        ) = refs[32:]
    n_dp, n_mp = axes
    me = lax.axis_index("mp")
    images, local, patches = img.shape
    units = tu.shape[1]
    chunk = images // 2
    pairs = chunk // 2
    width = n_mp * local
    quarter = patches // n_mp
    qrows = quarter * SUB
    half_p = patches // 2
    blocks = cu.shape[1] // width
    odd = lax.rem(me, 2)

    def peer(step):
        return lax.rem(me + step, n_mp)

    barrier = pltpu.get_barrier_semaphore()
    if fused:
        dp = lax.axis_index("dp")
        devices = n_dp * n_mp
        mine = dp * n_mp + me
        peers = devices - 1

        def device(number):
            return {"dp": number // n_mp, "mp": lax.rem(number, n_mp)}

        @pl.loop(1, devices)
        def _(step):
            other = lax.rem(mine + step, devices)
            pl.semaphore_signal(barrier, 1, device_id=device(other), device_id_type=pl.DeviceIdType.MESH)
    else:
        peers = n_mp - 1
        for step in range(1, n_mp):
            pl.semaphore_signal(barrier, 1, device_id={"mp": peer(step)}, device_id_type=pl.DeviceIdType.MESH)

    loads = [
        pltpu.make_async_copy(img_hbm, img, load_sem.at[0]),
        pltpu.make_async_copy(cd_hbm, cd, load_sem.at[1]),
        pltpu.make_async_copy(cot_hbm.at[:, pl.ds(0, chunk)], base.at[1], load_sem.at[2]),
        pltpu.make_async_copy(cot_hbm.at[:, pl.ds(chunk, chunk)], base.at[2], load_sem.at[3]),
        pltpu.make_async_copy(cu_hbm, cu, load_sem.at[4]),
    ]
    for load in loads:
        load.start()

    loads[0].wait()

    @pl.loop(0, images)
    def _(b):
        x = img[b].astype(F32)
        total = jnp.sum(x, 0, keepdims=True)
        center = x - total * (1.0 / local)
        stat_out[pl.ds(b, 1), :] = total
        stat_out[pl.ds(images + b, 1), :] = jnp.sum(center * center, 0, keepdims=True)

    def stat_copy(phase, step):
        return pltpu.make_async_remote_copy(
            src_ref=stat_out, dst_ref=stat_in.at[phase, me],
            send_sem=stat_send.at[phase, step - 1], recv_sem=stat_recv.at[phase, step - 1],
            device_id={"mp": peer(step)}, device_id_type=pl.DeviceIdType.MESH,
        )

    def share_stats(phase):
        stat_in[phase, me] = stat_out[...]
        for step in (2, 1, 3):
            stat_copy(phase, step).start()

    def wait_stats(phase):
        for step in range(1, n_mp):
            stat_copy(phase, step).wait()

    row = lax.broadcasted_iota(jnp.int32, (chunk, width), 0)
    for load in loads[2:4]:
        load.wait()

    def valid_of(h):
        return jnp.where(row + h * chunk < counts[0], 1.0, 0.0)[None]

    down_bias = jnp.zeros((chunk, width), F32)
    for h in range(2):
        masked = base[1 + h].astype(F32) * valid_of(h)
        base[1 + h] = masked.astype(BF)
        down_bias = down_bias + jnp.sum(masked, 0)
    down_bias = jnp.sum(down_bias, 0, keepdims=True)

    def flat(ref, i):
        return ref[i].reshape(quarter * chunk, width)

    def hidden_grads(h):
        @pl.loop(0, blocks)
        def _(block):
            cols = pl.ds(pl.multiple_of(block * width, width), width)
            grad = dot(flat(base, 1 + h), cd[cols, :], 1, 1).astype(BF)
            if h == 0:
                gbuf[1, block] = grad[:width].reshape(gbuf.shape[2:])
                dh_rest[block] = grad[width:]
            else:
                dh[block] = grad

    loads[1].wait()
    hidden_grads(0)
    pl.semaphore_wait(barrier, peers)
    share_stats(0)
    wait_stats(0)
    sums = [stat_in[0, k] for k in range(n_mp)]
    mean = sum(s[:images] for s in sums) * (1.0 / width)
    square = sum(s[images:] for s in sums)
    for s in sums:
        gap = s[:images] * (1.0 / local) - mean
        square = square + float(local) * (gap * gap)
    mean_inv[0] = mean
    mean_inv[1] = lax.rsqrt(square * (1.0 / width) + EPSILON)

    eye = jnp.where(
        lax.broadcasted_iota(jnp.int32, (patches, patches), 0)
        == lax.broadcasted_iota(jnp.int32, (patches, patches), 1), 1.0, 0.0,
    ).astype(BF)

    def line(ref):
        return ref[...].reshape(1, ref.shape[0])

    def columns(row):
        return jnp.transpose(jnp.broadcast_to(row, (128, 128)))

    for ref, col in ((pre_gain, gain_col), (pre_bias, bias_col)):
        values = line(ref)
        for i in range(width // 128):
            dn_acc[i * 128 : (i + 1) * 128, :128] = columns(values[:, i * 128 : (i + 1) * 128])
        start = pl.multiple_of(me * local, HALF)
        col[...] = dn_acc[pl.ds(start, local), :128]

    def lanes(ref):
        tile = ref[...]
        return jnp.concatenate([tile, tile], 1)[:, :patches]

    gain_one, bias_one = lanes(gain_col), lanes(bias_col)
    values = line(tdb)
    values = jnp.concatenate([values, jnp.zeros((1, 256 - patches), F32)], 1)
    column = jnp.concatenate([columns(values[:, :128]), columns(values[:, 128:])], 0)[:patches]
    token_down_bias = jnp.concatenate([column] * 3, 1)
    token_up_bias, mid_gain, mid_bias, down_bias_row = line(tub), line(mg), line(mb), line(cdb)

    def norm_of(b):
        return (img[b].astype(F32) - mean_inv[0, pl.ds(b, 1), :]) * mean_inv[1, pl.ds(b, 1), :]

    def slot_blocks(place):
        even = (0, 1, 2, 5, 3, 4)[place]
        other = (1, 2, 3, 0, 4, 5)[place]
        return even + odd * (other - even)

    def slot_rows(ref, q):
        rows = []
        for place in range(6):
            start = pl.multiple_of(slot_blocks(place) * HALF, HALF)
            rows.append(ref[q, pl.ds(start, HALF), :])
        return jnp.concatenate(rows, 0)

    def slot_images(b):
        rows = []
        for place in range(6):
            block = slot_blocks(place)
            which = block // 3
            start = pl.multiple_of((block - 3 * which) * HALF, HALF)
            rows.append(img[b + pairs * which, pl.ds(start, HALF), :])
        return jnp.concatenate(rows, 0)

    def forward_copy(h, step):
        return pltpu.make_async_remote_copy(
            src_ref=send.at[h, peer(step)], dst_ref=frecv.at[h, me],
            send_sem=f_send.at[h, step - 1], recv_sem=f_recv.at[h, step - 1],
            device_id={"mp": peer(step)}, device_id_type=pl.DeviceIdType.MESH,
        )

    def backward_copy(h, step):
        return pltpu.make_async_remote_copy(
            src_ref=send.at[h, peer(step)], dst_ref=frecv.at[h, me],
            send_sem=b_send.at[h, step - 1], recv_sem=b_recv.at[h, step - 1],
            device_id={"mp": peer(step)}, device_id_type=pl.DeviceIdType.MESH,
        )

    def group_images(h, i):
        return [h * chunk + i * GROUP + n + e * pairs for n in range(GROUP) for e in range(2)]

    def group_norm(h, i):
        norms = [norm_of(b) for b in group_images(h, i)]
        normed = [(norm * gain_one + bias_one).astype(BF) for norm in norms]
        return norms, jnp.concatenate(normed, 0)

    def group_slots():
        return jnp.concatenate([slot_rows(mixed, n) for n in range(GROUP)], 0)

    def token_forward(h):
        @pl.loop(0, pairs // GROUP)
        def _(i):
            _, normed = group_norm(h, i)
            mixed[...] = gelu(dot(normed, tu[...]) + token_up_bias).astype(BF).reshape(mixed.shape)
            held = [slot_images(h * chunk + i * GROUP + n) for n in range(GROUP)]
            out = dot(td[...], group_slots(), 1, 1) + dot(eye, jnp.concatenate(held, 0), 1, 1)
            out = out + jnp.concatenate([token_down_bias] * GROUP, 1)
            for n in range(GROUP):
                for t in range(3):
                    lanes_at = (3 * n + t) * 128
                    for side in range(2):
                        part = out[side * half_p : (side + 1) * half_p, lanes_at : lanes_at + 128]
                        stage[2 * t + side, pl.ds(i * GROUP + n, half_p, stride=SUB), :] = part

        for k in range(n_mp):
            for t in range(3):
                low_row = (k % 2) * qrows
                part = stage[2 * t + k // 2, low_row : low_row + qrows, :]
                send[h, k, :qrows, t * 128 : (t + 1) * 128] = part.astype(BF)
        frecv[h, me] = send[h, me]
        for step in (2, 1, 3):
            forward_copy(h, step).start()

    token_forward(0)
    token_forward(1)
    hidden_grads(1)

    low_half = lax.broadcasted_iota(jnp.int32, (1, 1, 128), 2) < HALF
    tiles = [(12 * i, 12) for i in range(quarter // 12)]
    tiles += [(12 * (quarter // 12), quarter % 12)] if quarter % 12 else []

    def arrived(ref, h, k, start, count):
        padded = count + count % 2
        rows = ref[h, k, start * SUB : (start + padded) * SUB, :].astype(F32)
        return rows[: count * SUB].reshape(count, SUB, 3 * 128)

    def tile(array, i):
        return array[:, :, i * 128 : (i + 1) * 128]

    def swap(array):
        count = array.shape[0]
        return pltpu.roll(array.reshape(count * SUB, 128), HALF, 1).reshape(count, SUB, 128)

    def merge(h, start, count):
        parts = [arrived(frecv, h, k, start, count) for k in range(n_mp)]
        first, second = [], []
        for k in range(0, n_mp, 2):
            a, b = parts[k], parts[k + 1]
            first += [tile(a, 0), jnp.where(low_half, tile(a, 1), tile(b, 1)), tile(b, 0)]
            second += [tile(a, 2), swap(jnp.where(low_half, tile(b, 1), tile(a, 1))), tile(b, 2)]
        rows = jnp.stack([jnp.concatenate(first, 2), jnp.concatenate(second, 2)], 1)
        return rows.reshape(count * 2 * SUB, width)

    def centered(x):
        center = x - jnp.sum(x, 1, keepdims=True) * (1.0 / width)
        spread_two = jnp.sum(center * center, 1, keepdims=True) * (1.0 / width)
        return center, lax.rsqrt(spread_two + EPSILON)

    def layer_norm_two(h):
        for start, count in tiles:
            rows = pl.ds(start * chunk, count * chunk)
            x = merge(h, start, count)
            mid[rows, :] = x.astype(BF)
            center, inv_two = centered(mid[rows, :].astype(F32))
            normed = (center * inv_two * mid_gain + mid_bias).astype(BF)
            base[0, start : start + count] = normed.reshape(count, chunk, width)

    def channel_block(h, block, between=None):
        cols = pl.ds(pl.multiple_of(block * width, width), width)
        if h == 0:
            grad = jnp.concatenate([gbuf[1, block].reshape(width, width), dh_rest[block]], 0)
        else:
            grad = dh[block]
        value, back = gelu_parts(dot(flat(base, 0), cu[:, cols]) + cub[cols].reshape(1, width))
        act[1] = value.astype(BF).reshape(quarter, chunk, width)
        pre = back * grad.astype(F32)
        up_bias[:, cols] += jnp.sum(pre.reshape(-1, SUB, width), 0)
        act[0] = pre.astype(BF).reshape(quarter, chunk, width)
        out = dot(flat(act, 1), cd[cols, :])
        for t in range(width // 128):
            stage[t] += out[:, t * 128 : (t + 1) * 128]
        dn_acc[...] += dot(flat(act, 0), cu[:, cols], 1, 1)
        if between is not None:
            between()
        for g, (left, right) in enumerate(((flat(act, 0), flat(base, 0)), (flat(act, 1), flat(base, 1 + h)))):
            part = dot(left, right, 0, 0).reshape(gbuf.shape[2:])
            if h > 0:
                part = part + gbuf[g, block].astype(F32)
            gbuf[g, block] = part.astype(BF)

    def finish_rows(h):
        gain_sum = jnp.zeros((SUB, width), F32)
        bias_sum = jnp.zeros((SUB, width), F32)
        valid = valid_of(h)
        for start, count in tiles:
            rows = pl.ds(start * chunk, count * chunk)
            x = mid[rows, :].astype(F32)
            out = jnp.concatenate([stage[t, rows, :] for t in range(width // 128)], 1)
            out = (x + out + down_bias_row).reshape(count, chunk, width) * valid
            act[1, start : start + count] = out.astype(BF)
            center, inv_two = centered(x)
            norm_two = center * inv_two
            dn = dn_acc[rows, :]
            gain_sum += jnp.sum((norm_two * dn).reshape(-1, SUB, width), 0)
            bias_sum += jnp.sum(dn.reshape(-1, SUB, width), 0)
            scaled = dn * mid_gain
            one = jnp.sum(scaled, 1, keepdims=True) * (1.0 / width)
            two = jnp.sum(scaled * norm_two, 1, keepdims=True) * (1.0 / width)
            grad = base[1 + h, start : start + count].reshape(count * chunk, width).astype(F32)
            grad = grad + inv_two * (scaled - one - norm_two * two)
            grad = grad.reshape(count, 2, SUB, width)
            first, second = grad[:, 0], grad[:, 1]
            for k in range(n_mp):
                left = 3 * (k // 2)
                if k % 2 == 0:
                    sides = (tile(first, left), tile(second, left))
                    middle = jnp.where(low_half, tile(first, left + 1), swap(tile(second, left + 1)))
                else:
                    sides = (tile(first, left + 2), tile(second, left + 2))
                    middle = jnp.where(low_half, swap(tile(second, left + 1)), tile(first, left + 1))
                rows_out = jnp.concatenate([sides[0], middle, sides[1]], 2)
                rows_out = rows_out.reshape(count * SUB, 3 * 128)
                if count % 2:
                    rows_out = jnp.concatenate([rows_out, jnp.zeros((SUB, 3 * 128), F32)], 0)
                send[h, k, start * SUB : (start + count + count % 2) * SUB, :] = rows_out.astype(BF)
        frecv[h, me] = send[h, me]
        return jnp.sum(gain_sum, 0, keepdims=True), jnp.sum(bias_sum, 0, keepdims=True)

    if fused:
        z, x = dp // 2, lax.rem(dp, 2)
        y, c = me // 2, odd

        def at(zz, xx, yy, cc):
            return {"dp": zz * 2 + xx, "mp": yy * 2 + cc}

        def block_at(t):
            return lax.rem(z + 1 + t, blocks)

        def remote(src, dst, sems, index, target):
            return pltpu.make_async_remote_copy(
                src_ref=src, dst_ref=dst, send_sem=sems.at[0, index], recv_sem=sems.at[1, index],
                device_id=target, device_id_type=pl.DeviceIdType.MESH,
            )

        def core_copy(t):
            return remote(gbuf.at[:, block_at(t), :, :, 1 - c], c_in, c_sem, 0, at(z, x, y, 1 - c))

        def xu_copy(t):
            return remote(gbuf.at[0, block_at(t), 1 - x, :, c], xu_in.at[t], x_sem, t, at(z, 1 - x, y, c))

        def yd_copy(t):
            if t < Y_FIRST:
                return remote(
                    gbuf.at[1, block_at(t), :, 1 - y, c], yd_in.at[t], y_sem, t, at(z, x, 1 - y, c)
                )
            return remote(gbuf.at[1, block_at(t), 1 - x, :, c], yd_in.at[t], y_sem, t, at(z, 1 - x, y, c))

        def xd_copy(t):
            if t < Y_FIRST:
                return remote(gbuf.at[1, block_at(t), 1 - x, y, c], xd_in.at[t], x2_sem, t, at(z, 1 - x, y, c))
            return remote(gbuf.at[1, block_at(t), x, 1 - y, c], xd_in.at[t], x2_sem, t, at(z, x, 1 - y, c))

        def zu_copy(t):
            return remote(gbuf.at[0, block_at(t), x, :, c], zu_in.at[t], zu_sem, t, at(block_at(t), x, y, c))

        def zd_copy(t):
            return remote(gbuf.at[1, block_at(t), x, y, c], zd_in.at[t], zd_sem, t, at(block_at(t), x, y, c))

        def add(ref, part):
            ref[...] = (ref[...].astype(F32) + part.astype(F32)).astype(BF)

        def end_core(t):
            core_copy(t).wait()
            for g in range(2):
                for xx in range(2):
                    for yy in range(2):
                        add(gbuf.at[g, block_at(t), xx, yy, c], c_in[g, xx, yy])

        def start_first(t):
            xu_copy(t).start()
            yd_copy(t).start()

        def end_first(t):
            xu_copy(t).wait()
            yd_copy(t).wait()
            for i in range(2):
                add(gbuf.at[0, block_at(t), x, i, c], xu_in[t, i])
                place = (i, y) if t < Y_FIRST else (x, i)
                add(gbuf.at[1, block_at(t), *place, c], yd_in[t, i])
            if t < blocks - 1:
                zu_copy(t).start()
            xd_copy(t).start()

        def end_second(t):
            xd_copy(t).wait()
            add(gbuf.at[1, block_at(t), x, y, c], xd_in[t])
            if t < blocks - 1:
                zd_copy(t).start()

        def scatter_step(t):
            end_core(t)
            start_first(t)
            if t < blocks - 1:
                pl.semaphore_signal(
                    core_credit, 1, device_id=at(z, x, y, 1 - c), device_id_type=pl.DeviceIdType.MESH
                )
                pl.semaphore_wait(core_credit, 1)
            if t >= 1:
                end_first(t - 1)
            if t >= 2:
                end_second(t - 2)

    def out_copy(h):
        return pltpu.make_async_copy(act.at[1], bo_hbm.at[:, pl.ds(h * chunk, chunk)], out_sem.at[h])

    def put(first_row, vector):
        for i in range(vector.shape[1] // 384):
            small[first_row + i : first_row + i + 1, :] = vector[:, i * 384 : (i + 1) * 384]

    small[...] = jnp.zeros_like(small)
    put(412, down_bias)
    loads[4].wait()
    totals = []

    def run_channel(h):
        for step in range(1, n_mp):
            forward_copy(h, step).wait()
        layer_norm_two(h)
        for step in range(1, n_mp):
            pl.semaphore_signal(
                credit.at[h], 1, device_id={"mp": peer(step)}, device_id_type=pl.DeviceIdType.MESH
            )
        stage[...] = jnp.zeros_like(stage)
        if h > 0:
            out_copy(0).wait()
        dn_acc[...] = jnp.zeros_like(dn_acc)

        if fused and h > 0:
            for t in range(blocks):
                channel_block(h, block_at(t), functools.partial(scatter_step, t - 1) if t else None)
                core_copy(t).start()
        else:

            @pl.loop(0, blocks)
            def _(t):
                channel_block(h, t)

        totals.append(finish_rows(h))
        pl.semaphore_wait(credit.at[h], n_mp - 1)
        for step in (2, 1, 3):
            backward_copy(h, step).start()
        out_copy(h).start()

    up_bias[...] = jnp.zeros_like(up_bias)
    run_channel(0)
    run_channel(1)
    put(400, jnp.sum(up_bias[...], 0, keepdims=True))
    put(408, totals[0][0] + totals[1][0])
    put(410, totals[0][1] + totals[1][1])
    last = blocks - 1
    if fused:
        scatter_step(last)
    else:
        grad_out = pltpu.make_async_copy(gbuf, gch_hbm, out_sem.at[2])
        grad_out.start()

    rows = lax.broadcasted_iota(jnp.int32, (HALF, 6 * HALF), 0)
    cols = lax.broadcasted_iota(jnp.int32, (HALF, 6 * HALF), 1)
    perm = jnp.zeros((6 * HALF, 6 * HALF), F32)
    all_rows = lax.broadcasted_iota(jnp.int32, (6 * HALF, 6 * HALF), 0)
    all_cols = lax.broadcasted_iota(jnp.int32, (6 * HALF, 6 * HALF), 1)
    for place in range(6):
        inside = (all_cols >= place * HALF) & (all_cols < (place + 1) * HALF)
        same = all_rows == all_cols + (slot_blocks(place) - place) * HALF
        perm = perm + jnp.where(inside & same, 1.0, 0.0)
    perm = perm.astype(BF)

    acc_g[...] = jnp.zeros_like(acc_g)
    acc_b[...] = jnp.zeros_like(acc_b)
    stat_out[...] = jnp.zeros_like(stat_out)

    def group_lanes(i, side):
        return pl.ds(pl.multiple_of((2 * i + side) * units, 128), units)

    def redo(h, i):
        _, normed = group_norm(h, i)
        value, back = gelu_parts(dot(normed, tu[...]) + token_up_bias)
        cu[:, group_lanes(i, 0)] = value.astype(BF)
        cu[:, group_lanes(i, 1)] = back.astype(BF)

    def kept_rows(i, n=0, count=2 * GROUP):
        return pl.ds(pl.multiple_of((2 * GROUP * i + n) * local, local), count * local)

    def weight_grads(h, i):
        slots, hidden_slots = [], []
        for n in range(GROUP):
            parts = [
                jnp.concatenate(
                    [stage[2 * t + k, pl.ds(i * GROUP + n, half_p, stride=SUB), :] for k in range(2)], 0
                )
                for t in range(3)
            ]
            slots.append(jnp.concatenate(parts, 1).astype(BF))
            for place in range(6):
                start = pl.multiple_of(2 * local * n + slot_blocks(place) * HALF, HALF)
                hidden_slots.append(cu[pl.ds(start, HALF), group_lanes(i, 0)])
        grad = jnp.concatenate([dot(perm, part, 1, 1) for part in slots], 0)
        low = grad.astype(BF)
        cd[kept_rows(i), 256 * h : 256 * h + patches] = low
        pre = cu[:, group_lanes(i, 1)].astype(F32) * dot(low, td[...])
        pre_low = pre.astype(BF)
        cu[:, group_lanes(i, 1)] = pre_low
        small[200 : 200 + patches, :] += dot(jnp.concatenate(slots, 1), jnp.concatenate(hidden_slots, 0))
        small[414:415, :] += jnp.sum(pre, 0, keepdims=True)
        small[415:416, :patches] += jnp.sum(grad, 0, keepdims=True)
        _, normed = group_norm(h, i)
        small[:patches, :] += dot(normed, pre_low, 0, 0)

    def input_grads(h, i):
        dn = dot(cu[:, group_lanes(i, 1)], tu[...], 1, 1)
        gain_sum, bias_sum = acc_g[...], acc_b[...]
        for n, b in enumerate(group_images(h, i)):
            part = dn[n * local : (n + 1) * local]
            prod = norm_of(b) * part
            gain_sum = gain_sum + prod
            bias_sum = bias_sum + part
            scaled = part * gain_one
            stat_out[pl.ds(b, 1), :] = jnp.sum(scaled, 0, keepdims=True)
            stat_out[pl.ds(images + b, 1), :] = jnp.sum(prod * gain_one, 0, keepdims=True)
            lanes_at = slice(256 * h, 256 * h + patches)
            kept = cd[kept_rows(i, n, 1), lanes_at].astype(F32) + mean_inv[1, pl.ds(b, 1), :] * scaled
            cd[kept_rows(i, n, 1), lanes_at] = kept.astype(BF)
        acc_g[...] = gain_sum
        acc_b[...] = bias_sum

    def collect(h):
        for step in range(1, n_mp):
            backward_copy(h, step).wait()
        for k in range(n_mp):
            for t in range(3):
                part = frecv[h, k, :qrows, t * 128 : (t + 1) * 128]
                low_row = (k % 2) * qrows
                stage[2 * t + k // 2, low_row : low_row + qrows, :] = part.astype(F32)

    def sweep(h, *passes):
        @pl.loop(0, pairs // GROUP)
        def _(i):
            for run in passes:
                run(h, i)

    collect(0)
    sweep(0, redo, weight_grads, input_grads)
    sweep(1, redo)
    if fused:
        end_second(last - 1)
    collect(1)
    sweep(1, weight_grads)
    if fused:
        part_out[:PARTS_EARLY] = small[: 16 * PARTS_EARLY, :].astype(BF).reshape(PARTS_EARLY, 16, units)

        def part_copy(step):
            other = lax.rem(mine + step, devices)
            return remote(part_out.at[other], part_in.at[step], part_sem, step, device(other))

        def whole_copy(step):
            other = lax.rem(mine + step, devices)
            return remote(part_out.at[mine], whole_in.at[mine], whole_sem, step, device(other))

        @pl.loop(1, devices)
        def _(step):
            @pl.when(lax.rem(mine + step, devices) < PARTS_EARLY)
            def _():
                part_copy(step).start()

        end_first(last)
    sweep(1, input_grads)
    share_stats(1)
    frame = []
    for acc in (acc_g, acc_b):
        column = jnp.broadcast_to(jnp.sum(acc[...], 1, keepdims=True), (local, 128))
        column = jnp.concatenate([column, jnp.zeros((256 - local, 128), F32)], 0)
        values = jnp.concatenate([jnp.transpose(column)[:SUB], jnp.zeros((SUB, 128), F32)], 1)
        values = jnp.where(odd > 0, pltpu.roll(values, local, 1), values)[:1]
        for i in range(n_mp // 2):
            frame.append(jnp.where(me // 2 == i, values, 0.0))
    if fused:
        frame = jnp.concatenate(frame + [jnp.zeros((12, units), F32)], 0)
        part_out[devices - n_mp + me] = frame.astype(BF)
        late_step = devices - n_mp - n_mp * dp

        @pl.when(dp < n_dp - 1)
        def _():
            part_copy(late_step).start()

        end_second(last)
        for step in range(last):
            zu_copy(step).wait()
        gu = [gbuf[0, z, x, i, c].astype(F32) for i in range(2)]
        for step in range(last):
            gu = [gu[i] + zu_in[step, i].astype(F32) for i in range(2)]
        y_out[...] = jnp.where(y > 0, gu[0], gu[1]).astype(BF)
        last_copy = remote(y_out, yu_in, y2_sem, 0, at(z, x, 1 - y, c))
        last_copy.start()
        cu_out[...] = jnp.where(y > 0, gu[1], gu[0])
        for step in range(last):
            zd_copy(step).wait()
        gd = gbuf[1, z, x, y, c].astype(F32)
        for step in range(last):
            gd = gd + zd_in[step].astype(F32)
        cd_out[...] = gd
    else:
        small[416:420, :] = jnp.concatenate(frame, 0)

    wait_stats(1)
    sums = [stat_in[1, k] for k in range(n_mp)]
    stat_out[...] = (sums[0] + sums[1] + sums[2] + sums[3]) * (1.0 / width)

    for h in range(2):

        @pl.loop(0, chunk)
        def _(i):
            b = h * chunk + lax.rem(i, 2) * pairs + i // 2
            one = stat_out[pl.ds(b, 1), :]
            two = stat_out[pl.ds(images + b, 1), :]
            first = pl.multiple_of(i * local, local)
            kept = cd[pl.ds(first, local), 256 * h : 256 * h + patches].astype(F32)
            grad = kept - mean_inv[1, pl.ds(b, 1), :] * (one + norm_of(b) * two)
            img[b] = grad.astype(BF)

    image_out = pltpu.make_async_copy(img, gi_hbm, out_sem.at[3])
    image_out.start()
    if fused:
        @pl.loop(1, devices)
        def _(step):
            other = lax.rem(mine + step, devices)

            @pl.when((other < PARTS_EARLY) | ((step == late_step) & (dp < n_dp - 1)))
            def _():
                part_copy(step).wait_send()

        @pl.when(mine < PARTS_EARLY)
        def _():
            @pl.loop(1, devices)
            def _(step):
                part_copy(step).wait_recv()

            total = part_out[mine].astype(F32)
            for step in range(1, devices):
                total = total + part_in[step].astype(F32)
            part_out[mine] = total.astype(BF)

        @pl.when(dp == n_dp - 1)
        def _():
            total = part_out[mine].astype(F32)
            for k in range(1, n_dp):
                part_copy(k * n_mp).wait_recv()
                total = total + part_in[k * n_mp].astype(F32)
            part_out[mine] = total.astype(BF)

        @pl.loop(1, devices)
        def _(step):
            whole_copy(step).start()

        whole_in[mine] = part_out[mine]
        last_copy.wait()
        cu_out[...] += yu_in[...].astype(F32)

        @pl.loop(1, devices)
        def _(step):
            whole_copy(step).wait()

        sums_out[...] = whole_in[...]
    else:
        small_out[...] = small[...]
        grad_out.wait()
    out_copy(1).wait()
    image_out.wait()


def unpack(
    bo_in, gi_in, sums, cu_in, cd_in,
    bo_out, gi_out, pg_out, pb_out, tu_out, tub_out, td_out, tdb_out, mg_out, mb_out,
    cu_out, cub_out, cd_out, cdb_out, small, bo, gi, cu, cd, sem,
):
    arrays = ((bo_in, bo_out, bo), (gi_in, gi_out, gi), (cu_in, cu_out, cu), (cd_in, cd_out, cd))
    arrivals, departures = [], []
    for i, (src, dst, held) in enumerate(arrays):
        count = held.shape[0]
        parts = PARTS if i < 2 else 1
        for part in range(parts):
            first, end = count * part // parts, count * (part + 1) // parts
            if i >= 2:
                first, end = 0, count
            rows = pl.ds(first, end - first)
            number = len(arrivals)
            arrivals.append(pltpu.make_async_copy(src.at[rows], held.at[rows], sem.at[0, number]))
            departures.append(pltpu.make_async_copy(held.at[rows], dst.at[rows], sem.at[1, number]))
    for copy in arrivals:
        copy.start()
    patches = tu_out.shape[0]
    small[...] = sums[...].astype(F32).reshape(small.shape)
    tu_out[...] = small[:patches, :]
    td_out[...] = small[200 : 200 + patches, :]

    def take(ref, first):
        count = ref.shape[0] // 384
        values = [small[first + i : first + i + 1, :] for i in range(count)]
        ref[...] = jnp.concatenate(values, 1).reshape(ref.shape)

    take(cub_out, 400)
    take(mg_out, 408)
    take(mb_out, 410)
    take(cdb_out, 412)
    take(tub_out, 414)
    tdb_out[...] = small[415:416, :patches].reshape(tdb_out.shape)
    for ref, first in ((pg_out, 448), (pb_out, 450)):
        values = [
            sum(small[first + 16 * k + i : first + 16 * k + i + 1, :] for k in range(4)) for i in range(2)
        ]
        ref[...] = jnp.concatenate(values, 1).reshape(ref.shape)
    for arrival, departure in zip(arrivals, departures):
        arrival.wait()
        departure.start()
    for departure in departures:
        departure.wait()


def shards(
    axes, images, counts, pre_gain, pre_bias, token_up, token_up_bias, token_down, token_down_bias,
    mid_gain, mid_bias, channel_up, channel_up_bias, channel_down, channel_down_bias, cotangent,
):
    n_dp, n_mp = axes
    count, patches, local = images.shape
    width, hidden = channel_up.shape
    units = token_up.shape[1]
    quarter = cotangent.shape[1]
    chunk = count // 2
    rows = quarter * chunk
    qpad = -(-quarter * SUB // 16) * 16
    fused = n_dp == 8 and n_mp == 4 and hidden == 4 * width
    unit = hidden // 32
    vector = [jax.ShapeDtypeStruct((n,), F32) for n in (width, hidden, units, patches)]
    table = jax.ShapeDtypeStruct((patches, units), F32)
    any_space = pl.BlockSpec(memory_space=pl.ANY)
    vmem = pl.BlockSpec(memory_space=pltpu.VMEM)
    smem = pl.BlockSpec(memory_space=pltpu.SMEM)
    V = pltpu.VMEM
    dma = pltpu.SemaphoreType.DMA
    if fused:
        slab = jax.ShapeDtypeStruct((unit, width), F32)
        grads = (jax.ShapeDtypeStruct((32, 16, units), BF), slab, slab)
        grad_specs = (vmem,) * 3
    else:
        grads = (
            jax.ShapeDtypeStruct((2, hidden // width, 2, 2, 2, unit, width), BF),
            jax.ShapeDtypeStruct((512, units), F32),
        )
        grad_specs = (any_space, vmem)
    pair = dma((2, n_mp - 1))
    extra = [
        V((2, 2, 2, unit, width), BF),
        V((4, 2, unit, width), BF),
        V((4, 2, unit, width), BF),
        V((4, unit, width), BF),
        V((3, 2, unit, width), BF),
        V((3, unit, width), BF),
        V((unit, width), BF),
        V((unit, width), BF),
        V((32, 16, units), BF),
        V((32, 16, units), BF),
        V((32, 16, units), BF),
        dma((2, 1)),
        dma((2, 4)),
        dma((2, 4)),
        dma((2, 4)),
        dma((2, 3)),
        dma((2, 3)),
        dma((2, 1)),
        dma((2, 32)),
        dma((2, 32)),
        pltpu.SemaphoreType.REGULAR,
    ]
    out = pl.pallas_call(
        functools.partial(kernel, axes, fused),
        out_shape=(
            jax.ShapeDtypeStruct((quarter, count, width), BF),
            jax.ShapeDtypeStruct((count, local, patches), BF),
        )
        + grads,
        in_specs=[smem] + [any_space] * 4 + [vmem] * 10,
        out_specs=(any_space, any_space) + grad_specs,
        scratch_shapes=[
            V((count, local, patches), BF),
            V((width, hidden), BF),
            V((hidden, width), BF),
            V((3, quarter, chunk, width), BF),
            V((hidden // width, rows, width), BF),
            V((hidden // width, rows - width, width), BF),
            V((2 * count, patches), F32),
            V((2, n_mp, 2 * count, patches), F32),
            V((2, count, patches), F32),
            V((GROUP, 2 * local, units), BF),
            V((width // 128, rows, 128), F32),
            V((2, n_mp, qpad, 2 * local), BF),
            V((2, n_mp, qpad, 2 * local), BF),
            V((rows, width), BF),
            V((2, quarter, chunk, width), BF),
            V((rows, width), F32),
            V((2, hidden // width, 2, 2, 2, unit, width), BF),
            V((local, patches), F32),
            V((local, patches), F32),
            V((SUB, hidden), F32),
            V((512, units), F32),
            V((local, 128), F32),
            V((local, 128), F32),
            dma((5,)),
            dma((4,)),
            pair,
            pair,
            pair,
            pair,
            pair,
            pair,
            pltpu.SemaphoreType.REGULAR((2,)),
        ]
        + (extra if fused else []),
        compiler_params=pltpu.CompilerParams(
            collective_id=0, has_side_effects=True, vmem_limit_bytes=64 * 2**20 - 2**17
        ),
    )(
        counts,
        jnp.transpose(images, (0, 2, 1)),
        jnp.transpose(cotangent, (1, 0, 2)),
        channel_up,
        channel_down,
        token_up,
        jnp.transpose(token_down),
        pre_gain,
        pre_bias,
        token_up_bias,
        token_down_bias,
        mid_gain,
        mid_bias,
        channel_up_bias,
        channel_down_bias,
    )
    if fused:
        finals = list(vector[:1] * 2 + [table, vector[2], table, vector[3]] + vector[:1] * 2)
        finals += [slab, vector[1], slab, vector[0]]
        rest = pl.pallas_call(
            unpack,
            out_shape=tuple(jax.ShapeDtypeStruct(o.shape, o.dtype) for o in out[:2]) + tuple(finals),
            in_specs=[any_space] * 2 + [vmem] + [any_space] * 2,
            out_specs=(any_space, any_space) + (vmem,) * 8 + (any_space, vmem, any_space, vmem),
            scratch_shapes=[V((512, units), F32)]
            + [V(o.shape, o.dtype) for o in (*out[:2], *out[3:])]
            + [dma((2, 2 * PARTS + 2))],
            compiler_params=pltpu.CompilerParams(vmem_limit_bytes=60 * 2**20),
        )(*out)
        rest = list(rest)
        rest[0] = jnp.transpose(rest[0], (1, 0, 2))
        rest[1] = jnp.transpose(rest[1], (0, 2, 1))
        rest[6] = jnp.transpose(rest[6])
        rest[10] = jnp.transpose(rest[10])
        return tuple(rest)
    block_out, grad_images = jnp.transpose(out[0], (1, 0, 2)), jnp.transpose(out[1], (0, 2, 1))
    both = ("dp", "mp")
    grads = out[2].reshape(2, hidden, width).astype(F32)
    wide = lax.psum_scatter(grads, both, scatter_dimension=1, tiled=True)
    small = lax.psum(out[3], both)
    return (
        block_out,
        grad_images,
        small[416:418].reshape(width),
        small[418:420].reshape(width),
        small[:patches],
        small[414],
        jnp.transpose(small[200 : 200 + patches]),
        small[415, :patches],
        small[408:410].reshape(width),
        small[410:412].reshape(width),
        jnp.transpose(wide[0]),
        small[400:408].reshape(hidden),
        wide[1],
        small[412:414].reshape(width),
    )


def solution(mesh):
    axes = (mesh.shape["dp"], mesh.shape["mp"])
    in_specs = (P("dp", None, "mp"), P("dp")) + (P(),) * 12 + (P("dp", "mp", None),)
    out_specs = (
        (P("dp", "mp", None), P("dp", None, "mp"))
        + (P(),) * 8
        + (P(None, ("dp", "mp")), P(), P(("dp", "mp"), None), P())
    )
    return jax.shard_map(
        functools.partial(shards, axes), mesh=mesh, in_specs=in_specs, out_specs=out_specs, check_vma=False
    )
```

```python
import functools

import jax
import jax.numpy as jnp
from jax import lax
from jax.experimental import pallas as pl
from jax.experimental.pallas import tpu as pltpu
from jax.sharding import PartitionSpec as P

EPSILON = 1e-06
GELU_ROOT = 0.7978845608028654
GELU_CUBE = 0.044715
BF = jnp.bfloat16
F32 = jnp.float32
HALF = 64
SUB = 8
PARTS = 7
PARTS_EARLY = 27
GROUP = 2


def dot(left, right, left_dim=1, right_dim=0):
    return lax.dot_general(
        left, right, (((left_dim,), (right_dim,)), ((), ())), preferred_element_type=F32
    )


def gelu(x):
    half = 0.5 * x
    return half + half * jnp.tanh(x * (x * x * (GELU_ROOT * GELU_CUBE) + GELU_ROOT))


def gelu_parts(x):
    squares = x * x
    slope = squares * (GELU_ROOT * GELU_CUBE) + GELU_ROOT
    t = jnp.tanh(x * slope)
    half = 0.5 * x
    value = half + half * t
    inner = slope + squares * (2.0 * GELU_ROOT * GELU_CUBE)
    back = (0.5 + 0.5 * t) + (half * inner) * (1.0 - t * t)
    return value, back


def kernel(axes, fused, *refs):
    (
        counts, img_hbm, cot_hbm, cu_hbm, cd_hbm, tu, td, pre_gain, pre_bias, tub, tdb, mg, mb, cub, cdb,
    ) = refs[:15]
    refs = refs[15:]
    bo_hbm, gi_hbm = refs[:2]
    if fused:
        sums_out, cu_out, cd_out = refs[2:5]
        refs = refs[5:]
    else:
        gch_hbm, small_out = refs[2:4]
        refs = refs[4:]
    (
        img, cu, cd, base, dh, dh_rest, stat_out, stat_in, mean_inv, mixed, stage, send, frecv,
        mid, act, dn_acc, gbuf, acc_g, acc_b, up_bias, small, gain_col, bias_col,
        load_sem, out_sem, stat_send, stat_recv, f_send, f_recv, b_send, b_recv, credit,
    ) = refs[:32]
    if fused:
        (
            c_in, xu_in, yd_in, xd_in, zu_in, zd_in, yu_in, y_out, part_out, part_in, whole_in,
            c_sem, x_sem, y_sem, x2_sem, zu_sem, zd_sem, y2_sem, part_sem, whole_sem, core_credit,
        ) = refs[32:]
    n_dp, n_mp = axes
    me = lax.axis_index("mp")
    images, local, patches = img.shape
    units = tu.shape[1]
    chunk = images // 2
    pairs = chunk // 2
    width = n_mp * local
    quarter = patches // n_mp
    qrows = quarter * SUB
    half_p = patches // 2
    blocks = cu.shape[1] // width
    odd = lax.rem(me, 2)

    def peer(step):
        return lax.rem(me + step, n_mp)

    barrier = pltpu.get_barrier_semaphore()
    if fused:
        dp = lax.axis_index("dp")
        devices = n_dp * n_mp
        mine = dp * n_mp + me
        peers = devices - 1

        def device(number):
            return {"dp": number // n_mp, "mp": lax.rem(number, n_mp)}

        @pl.loop(1, devices)
        def _(step):
            other = lax.rem(mine + step, devices)
            pl.semaphore_signal(barrier, 1, device_id=device(other), device_id_type=pl.DeviceIdType.MESH)
    else:
        peers = n_mp - 1
        for step in range(1, n_mp):
            pl.semaphore_signal(barrier, 1, device_id={"mp": peer(step)}, device_id_type=pl.DeviceIdType.MESH)

    loads = [
        pltpu.make_async_copy(img_hbm, img, load_sem.at[0]),
        pltpu.make_async_copy(cd_hbm, cd, load_sem.at[1]),
        pltpu.make_async_copy(cot_hbm.at[:, pl.ds(0, chunk)], base.at[1], load_sem.at[2]),
        pltpu.make_async_copy(cot_hbm.at[:, pl.ds(chunk, chunk)], base.at[2], load_sem.at[3]),
        pltpu.make_async_copy(cu_hbm, cu, load_sem.at[4]),
    ]
    for load in loads:
        load.start()

    loads[0].wait()

    @pl.loop(0, images)
    def _(b):
        x = img[b].astype(F32)
        total = jnp.sum(x, 0, keepdims=True)
        center = x - total * (1.0 / local)
        stat_out[pl.ds(b, 1), :] = total
        stat_out[pl.ds(images + b, 1), :] = jnp.sum(center * center, 0, keepdims=True)

    def stat_copy(phase, step):
        return pltpu.make_async_remote_copy(
            src_ref=stat_out, dst_ref=stat_in.at[phase, me],
            send_sem=stat_send.at[phase, step - 1], recv_sem=stat_recv.at[phase, step - 1],
            device_id={"mp": peer(step)}, device_id_type=pl.DeviceIdType.MESH,
        )

    def share_stats(phase):
        stat_in[phase, me] = stat_out[...]
        for step in (2, 1, 3):
            stat_copy(phase, step).start()

    def wait_stats(phase):
        for step in range(1, n_mp):
            stat_copy(phase, step).wait()

    row = lax.broadcasted_iota(jnp.int32, (chunk, width), 0)
    for load in loads[2:4]:
        load.wait()

    def valid_of(h):
        return jnp.where(row + h * chunk < counts[0], 1.0, 0.0)[None]

    down_bias = jnp.zeros((chunk, width), F32)
    for h in range(2):
        masked = base[1 + h].astype(F32) * valid_of(h)
        base[1 + h] = masked.astype(BF)
        down_bias = down_bias + jnp.sum(masked, 0)
    down_bias = jnp.sum(down_bias, 0, keepdims=True)

    def flat(ref, i):
        return ref[i].reshape(quarter * chunk, width)

    def hidden_grads(h):
        @pl.loop(0, blocks)
        def _(block):
            cols = pl.ds(pl.multiple_of(block * width, width), width)
            grad = dot(flat(base, 1 + h), cd[cols, :], 1, 1).astype(BF)
            if h == 0:
                gbuf[1, block] = grad[:width].reshape(gbuf.shape[2:])
                dh_rest[block] = grad[width:]
            else:
                dh[block] = grad

    loads[1].wait()
    hidden_grads(0)
    pl.semaphore_wait(barrier, peers)
    share_stats(0)
    wait_stats(0)
    sums = [stat_in[0, k] for k in range(n_mp)]
    mean = sum(s[:images] for s in sums) * (1.0 / width)
    square = sum(s[images:] for s in sums)
    for s in sums:
        gap = s[:images] * (1.0 / local) - mean
        square = square + float(local) * (gap * gap)
    mean_inv[0] = mean
    mean_inv[1] = lax.rsqrt(square * (1.0 / width) + EPSILON)

    eye = jnp.where(
        lax.broadcasted_iota(jnp.int32, (patches, patches), 0)
        == lax.broadcasted_iota(jnp.int32, (patches, patches), 1), 1.0, 0.0,
    ).astype(BF)

    def line(ref):
        return ref[...].reshape(1, ref.shape[0])

    def columns(row):
        return jnp.transpose(jnp.broadcast_to(row, (128, 128)))

    for ref, col in ((pre_gain, gain_col), (pre_bias, bias_col)):
        values = line(ref)
        for i in range(width // 128):
            dn_acc[i * 128 : (i + 1) * 128, :128] = columns(values[:, i * 128 : (i + 1) * 128])
        start = pl.multiple_of(me * local, HALF)
        col[...] = dn_acc[pl.ds(start, local), :128]

    def lanes(ref):
        tile = ref[...]
        return jnp.concatenate([tile, tile], 1)[:, :patches]

    gain_one, bias_one = lanes(gain_col), lanes(bias_col)
    values = line(tdb)
    values = jnp.concatenate([values, jnp.zeros((1, 256 - patches), F32)], 1)
    column = jnp.concatenate([columns(values[:, :128]), columns(values[:, 128:])], 0)[:patches]
    token_down_bias = jnp.concatenate([column] * 3, 1)
    token_up_bias, mid_gain, mid_bias, down_bias_row = line(tub), line(mg), line(mb), line(cdb)

    def norm_of(b):
        return (img[b].astype(F32) - mean_inv[0, pl.ds(b, 1), :]) * mean_inv[1, pl.ds(b, 1), :]

    def slot_blocks(place):
        even = (0, 1, 2, 5, 3, 4)[place]
        other = (1, 2, 3, 0, 4, 5)[place]
        return even + odd * (other - even)

    def slot_rows(ref, q):
        rows = []
        for place in range(6):
            start = pl.multiple_of(slot_blocks(place) * HALF, HALF)
            rows.append(ref[q, pl.ds(start, HALF), :])
        return jnp.concatenate(rows, 0)

    def slot_images(b):
        rows = []
        for place in range(6):
            block = slot_blocks(place)
            which = block // 3
            start = pl.multiple_of((block - 3 * which) * HALF, HALF)
            rows.append(img[b + pairs * which, pl.ds(start, HALF), :])
        return jnp.concatenate(rows, 0)

    def forward_copy(h, step):
        return pltpu.make_async_remote_copy(
            src_ref=send.at[h, peer(step)], dst_ref=frecv.at[h, me],
            send_sem=f_send.at[h, step - 1], recv_sem=f_recv.at[h, step - 1],
            device_id={"mp": peer(step)}, device_id_type=pl.DeviceIdType.MESH,
        )

    def backward_copy(h, step):
        return pltpu.make_async_remote_copy(
            src_ref=send.at[h, peer(step)], dst_ref=frecv.at[h, me],
            send_sem=b_send.at[h, step - 1], recv_sem=b_recv.at[h, step - 1],
            device_id={"mp": peer(step)}, device_id_type=pl.DeviceIdType.MESH,
        )

    def group_images(h, i):
        return [h * chunk + i * GROUP + n + e * pairs for n in range(GROUP) for e in range(2)]

    def group_norm(h, i):
        norms = [norm_of(b) for b in group_images(h, i)]
        normed = [(norm * gain_one + bias_one).astype(BF) for norm in norms]
        return norms, jnp.concatenate(normed, 0)

    def group_slots():
        return jnp.concatenate([slot_rows(mixed, n) for n in range(GROUP)], 0)

    def token_forward(h):
        @pl.loop(0, pairs // GROUP)
        def _(i):
            _, normed = group_norm(h, i)
            mixed[...] = gelu(dot(normed, tu[...]) + token_up_bias).astype(BF).reshape(mixed.shape)
            held = [slot_images(h * chunk + i * GROUP + n) for n in range(GROUP)]
            out = dot(td[...], group_slots(), 1, 1) + dot(eye, jnp.concatenate(held, 0), 1, 1)
            out = out + jnp.concatenate([token_down_bias] * GROUP, 1)
            for n in range(GROUP):
                for t in range(3):
                    lanes_at = (3 * n + t) * 128
                    for side in range(2):
                        part = out[side * half_p : (side + 1) * half_p, lanes_at : lanes_at + 128]
                        stage[2 * t + side, pl.ds(i * GROUP + n, half_p, stride=SUB), :] = part

        for k in range(n_mp):
            for t in range(3):
                low_row = (k % 2) * qrows
                part = stage[2 * t + k // 2, low_row : low_row + qrows, :]
                send[h, k, :qrows, t * 128 : (t + 1) * 128] = part.astype(BF)
        frecv[h, me] = send[h, me]
        for step in (2, 1, 3):
            forward_copy(h, step).start()

    token_forward(0)
    token_forward(1)
    hidden_grads(1)

    low_half = lax.broadcasted_iota(jnp.int32, (1, 1, 128), 2) < HALF
    tiles = [(12 * i, 12) for i in range(quarter // 12)]
    tiles += [(12 * (quarter // 12), quarter % 12)] if quarter % 12 else []

    def arrived(ref, h, k, start, count):
        padded = count + count % 2
        rows = ref[h, k, start * SUB : (start + padded) * SUB, :].astype(F32)
        return rows[: count * SUB].reshape(count, SUB, 3 * 128)

    def tile(array, i):
        return array[:, :, i * 128 : (i + 1) * 128]

    def swap(array):
        count = array.shape[0]
        return pltpu.roll(array.reshape(count * SUB, 128), HALF, 1).reshape(count, SUB, 128)

    def merge(h, start, count):
        parts = [arrived(frecv, h, k, start, count) for k in range(n_mp)]
        first, second = [], []
        for k in range(0, n_mp, 2):
            a, b = parts[k], parts[k + 1]
            first += [tile(a, 0), jnp.where(low_half, tile(a, 1), tile(b, 1)), tile(b, 0)]
            second += [tile(a, 2), swap(jnp.where(low_half, tile(b, 1), tile(a, 1))), tile(b, 2)]
        rows = jnp.stack([jnp.concatenate(first, 2), jnp.concatenate(second, 2)], 1)
        return rows.reshape(count * 2 * SUB, width)

    def centered(x):
        center = x - jnp.sum(x, 1, keepdims=True) * (1.0 / width)
        spread_two = jnp.sum(center * center, 1, keepdims=True) * (1.0 / width)
        return center, lax.rsqrt(spread_two + EPSILON)

    def layer_norm_two(h):
        for start, count in tiles:
            rows = pl.ds(start * chunk, count * chunk)
            x = merge(h, start, count)
            mid[rows, :] = x.astype(BF)
            center, inv_two = centered(mid[rows, :].astype(F32))
            normed = (center * inv_two * mid_gain + mid_bias).astype(BF)
            base[0, start : start + count] = normed.reshape(count, chunk, width)

    def channel_block(h, block, between=None):
        cols = pl.ds(pl.multiple_of(block * width, width), width)
        if h == 0:
            grad = jnp.concatenate([gbuf[1, block].reshape(width, width), dh_rest[block]], 0)
        else:
            grad = dh[block]
        value, back = gelu_parts(dot(flat(base, 0), cu[:, cols]) + cub[cols].reshape(1, width))
        act[1] = value.astype(BF).reshape(quarter, chunk, width)
        pre = back * grad.astype(F32)
        up_bias[:, cols] += jnp.sum(pre.reshape(-1, SUB, width), 0)
        act[0] = pre.astype(BF).reshape(quarter, chunk, width)
        out = dot(flat(act, 1), cd[cols, :])
        for t in range(width // 128):
            stage[t] += out[:, t * 128 : (t + 1) * 128]
        dn_acc[...] += dot(flat(act, 0), cu[:, cols], 1, 1)
        if between is not None:
            between()
        for g, (left, right) in enumerate(((flat(act, 0), flat(base, 0)), (flat(act, 1), flat(base, 1 + h)))):
            part = dot(left, right, 0, 0).reshape(gbuf.shape[2:])
            if h > 0:
                part = part + gbuf[g, block].astype(F32)
            gbuf[g, block] = part.astype(BF)

    def finish_rows(h):
        gain_sum = jnp.zeros((SUB, width), F32)
        bias_sum = jnp.zeros((SUB, width), F32)
        valid = valid_of(h)
        for start, count in tiles:
            rows = pl.ds(start * chunk, count * chunk)
            x = mid[rows, :].astype(F32)
            out = jnp.concatenate([stage[t, rows, :] for t in range(width // 128)], 1)
            out = (x + out + down_bias_row).reshape(count, chunk, width) * valid
            act[1, start : start + count] = out.astype(BF)
            center, inv_two = centered(x)
            norm_two = center * inv_two
            dn = dn_acc[rows, :]
            gain_sum += jnp.sum((norm_two * dn).reshape(-1, SUB, width), 0)
            bias_sum += jnp.sum(dn.reshape(-1, SUB, width), 0)
            scaled = dn * mid_gain
            one = jnp.sum(scaled, 1, keepdims=True) * (1.0 / width)
            two = jnp.sum(scaled * norm_two, 1, keepdims=True) * (1.0 / width)
            grad = base[1 + h, start : start + count].reshape(count * chunk, width).astype(F32)
            grad = grad + inv_two * (scaled - one - norm_two * two)
            grad = grad.reshape(count, 2, SUB, width)
            first, second = grad[:, 0], grad[:, 1]
            for k in range(n_mp):
                left = 3 * (k // 2)
                if k % 2 == 0:
                    sides = (tile(first, left), tile(second, left))
                    middle = jnp.where(low_half, tile(first, left + 1), swap(tile(second, left + 1)))
                else:
                    sides = (tile(first, left + 2), tile(second, left + 2))
                    middle = jnp.where(low_half, swap(tile(second, left + 1)), tile(first, left + 1))
                rows_out = jnp.concatenate([sides[0], middle, sides[1]], 2)
                rows_out = rows_out.reshape(count * SUB, 3 * 128)
                if count % 2:
                    rows_out = jnp.concatenate([rows_out, jnp.zeros((SUB, 3 * 128), F32)], 0)
                send[h, k, start * SUB : (start + count + count % 2) * SUB, :] = rows_out.astype(BF)
        frecv[h, me] = send[h, me]
        return jnp.sum(gain_sum, 0, keepdims=True), jnp.sum(bias_sum, 0, keepdims=True)

    if fused:
        z, x = dp // 2, lax.rem(dp, 2)
        y, c = me // 2, odd

        def at(zz, xx, yy, cc):
            return {"dp": zz * 2 + xx, "mp": yy * 2 + cc}

        def block_at(t):
            return lax.rem(z + 1 + t, blocks)

        def remote(src, dst, sems, index, target):
            return pltpu.make_async_remote_copy(
                src_ref=src, dst_ref=dst, send_sem=sems.at[0, index], recv_sem=sems.at[1, index],
                device_id=target, device_id_type=pl.DeviceIdType.MESH,
            )

        def core_copy(t):
            return remote(gbuf.at[:, block_at(t), :, :, 1 - c], c_in, c_sem, 0, at(z, x, y, 1 - c))

        def xu_copy(t):
            return remote(gbuf.at[0, block_at(t), 1 - x, :, c], xu_in.at[t], x_sem, t, at(z, 1 - x, y, c))

        def yd_copy(t):
            return remote(gbuf.at[1, block_at(t), :, 1 - y, c], yd_in.at[t], y_sem, t, at(z, x, 1 - y, c))

        def xd_copy(t):
            return remote(gbuf.at[1, block_at(t), 1 - x, y, c], xd_in.at[t], x2_sem, t, at(z, 1 - x, y, c))

        def zu_copy(t):
            return remote(gbuf.at[0, block_at(t), x, :, c], zu_in.at[t], zu_sem, t, at(block_at(t), x, y, c))

        def zd_copy(t):
            return remote(gbuf.at[1, block_at(t), x, y, c], zd_in.at[t], zd_sem, t, at(block_at(t), x, y, c))

        def add(ref, part):
            ref[...] = (ref[...].astype(F32) + part.astype(F32)).astype(BF)

        def end_core(t):
            core_copy(t).wait()
            for g in range(2):
                for xx in range(2):
                    for yy in range(2):
                        add(gbuf.at[g, block_at(t), xx, yy, c], c_in[g, xx, yy])

        def start_first(t):
            xu_copy(t).start()
            yd_copy(t).start()

        def end_first(t):
            xu_copy(t).wait()
            yd_copy(t).wait()
            for i in range(2):
                add(gbuf.at[0, block_at(t), x, i, c], xu_in[t, i])
                add(gbuf.at[1, block_at(t), i, y, c], yd_in[t, i])
            if not isinstance(t, int) or t < blocks - 1:
                zu_copy(t).start()
            xd_copy(t).start()

        def end_second(t):
            xd_copy(t).wait()
            add(gbuf.at[1, block_at(t), x, y, c], xd_in[t])
            if not isinstance(t, int) or t < blocks - 1:
                zd_copy(t).start()

        def scatter_step(t):
            end_core(t)
            start_first(t)
            if isinstance(t, int):
                end_first(t - 1)
                end_second(t - 2)
                return
            pl.semaphore_signal(
                core_credit, 1, device_id=at(z, x, y, 1 - c), device_id_type=pl.DeviceIdType.MESH
            )
            pl.semaphore_wait(core_credit, 1)

            @pl.when(t >= 1)
            def _():
                end_first(t - 1)

            @pl.when(t >= 2)
            def _():
                end_second(t - 2)

    def out_copy(h):
        return pltpu.make_async_copy(act.at[1], bo_hbm.at[:, pl.ds(h * chunk, chunk)], out_sem.at[h])

    def put(first_row, vector):
        for i in range(vector.shape[1] // 384):
            small[first_row + i : first_row + i + 1, :] = vector[:, i * 384 : (i + 1) * 384]

    small[...] = jnp.zeros_like(small)
    put(412, down_bias)
    loads[4].wait()
    totals = []

    def run_channel(h):
        for step in range(1, n_mp):
            forward_copy(h, step).wait()
        layer_norm_two(h)
        for step in range(1, n_mp):
            pl.semaphore_signal(
                credit.at[h], 1, device_id={"mp": peer(step)}, device_id_type=pl.DeviceIdType.MESH
            )
        stage[...] = jnp.zeros_like(stage)
        if h > 0:
            out_copy(0).wait()
        dn_acc[...] = jnp.zeros_like(dn_acc)

        if fused and h > 0:


            @pl.loop(0, blocks)
            def _(t):
                def between():
                    @pl.when(t >= 1)
                    def _():
                        scatter_step(t - 1)

                channel_block(h, block_at(t), between)
                core_copy(t).start()

        else:

            @pl.loop(0, blocks)
            def _(t):
                channel_block(h, t)

        totals.append(finish_rows(h))
        pl.semaphore_wait(credit.at[h], n_mp - 1)
        for step in (2, 1, 3):
            backward_copy(h, step).start()
        out_copy(h).start()

    up_bias[...] = jnp.zeros_like(up_bias)
    run_channel(0)
    run_channel(1)
    put(400, jnp.sum(up_bias[...], 0, keepdims=True))
    put(408, totals[0][0] + totals[1][0])
    put(410, totals[0][1] + totals[1][1])
    last = blocks - 1
    if fused:
        scatter_step(last)
    else:
        grad_out = pltpu.make_async_copy(gbuf, gch_hbm, out_sem.at[2])
        grad_out.start()

    rows = lax.broadcasted_iota(jnp.int32, (HALF, 6 * HALF), 0)
    cols = lax.broadcasted_iota(jnp.int32, (HALF, 6 * HALF), 1)
    perm = jnp.zeros((6 * HALF, 6 * HALF), F32)
    all_rows = lax.broadcasted_iota(jnp.int32, (6 * HALF, 6 * HALF), 0)
    all_cols = lax.broadcasted_iota(jnp.int32, (6 * HALF, 6 * HALF), 1)
    for place in range(6):
        inside = (all_cols >= place * HALF) & (all_cols < (place + 1) * HALF)
        same = all_rows == all_cols + (slot_blocks(place) - place) * HALF
        perm = perm + jnp.where(inside & same, 1.0, 0.0)
    perm = perm.astype(BF)

    acc_g[...] = jnp.zeros_like(acc_g)
    acc_b[...] = jnp.zeros_like(acc_b)
    stat_out[...] = jnp.zeros_like(stat_out)

    def group_lanes(i, side):
        return pl.ds(pl.multiple_of((2 * i + side) * units, 128), units)

    def redo(h, i):
        _, normed = group_norm(h, i)
        value, back = gelu_parts(dot(normed, tu[...]) + token_up_bias)
        cu[:, group_lanes(i, 0)] = value.astype(BF)
        cu[:, group_lanes(i, 1)] = back.astype(BF)

    def kept_rows(i, n=0, count=2 * GROUP):
        return pl.ds(pl.multiple_of((2 * GROUP * i + n) * local, local), count * local)

    def weight_grads(h, i):
        slots, hidden_slots = [], []
        for n in range(GROUP):
            parts = [
                jnp.concatenate(
                    [stage[2 * t + k, pl.ds(i * GROUP + n, half_p, stride=SUB), :] for k in range(2)], 0
                )
                for t in range(3)
            ]
            slots.append(jnp.concatenate(parts, 1).astype(BF))
            for place in range(6):
                start = pl.multiple_of(2 * local * n + slot_blocks(place) * HALF, HALF)
                hidden_slots.append(cu[pl.ds(start, HALF), group_lanes(i, 0)])
        grad = jnp.concatenate([dot(perm, part, 1, 1) for part in slots], 0)
        low = grad.astype(BF)
        cd[kept_rows(i), 256 * h : 256 * h + patches] = low
        pre = cu[:, group_lanes(i, 1)].astype(F32) * dot(low, td[...])
        pre_low = pre.astype(BF)
        cu[:, group_lanes(i, 1)] = pre_low
        small[200 : 200 + patches, :] += dot(jnp.concatenate(slots, 1), jnp.concatenate(hidden_slots, 0))
        small[414:415, :] += jnp.sum(pre, 0, keepdims=True)
        small[415:416, :patches] += jnp.sum(grad, 0, keepdims=True)
        _, normed = group_norm(h, i)
        small[:patches, :] += dot(normed, pre_low, 0, 0)

    def input_grads(h, i):
        dn = dot(cu[:, group_lanes(i, 1)], tu[...], 1, 1)
        gain_sum, bias_sum = acc_g[...], acc_b[...]
        for n, b in enumerate(group_images(h, i)):
            part = dn[n * local : (n + 1) * local]
            prod = norm_of(b) * part
            gain_sum = gain_sum + prod
            bias_sum = bias_sum + part
            scaled = part * gain_one
            stat_out[pl.ds(b, 1), :] = jnp.sum(scaled, 0, keepdims=True)
            stat_out[pl.ds(images + b, 1), :] = jnp.sum(prod * gain_one, 0, keepdims=True)
            lanes_at = slice(256 * h, 256 * h + patches)
            kept = cd[kept_rows(i, n, 1), lanes_at].astype(F32) + mean_inv[1, pl.ds(b, 1), :] * scaled
            cd[kept_rows(i, n, 1), lanes_at] = kept.astype(BF)
        acc_g[...] = gain_sum
        acc_b[...] = bias_sum

    def collect(h):
        for step in range(1, n_mp):
            backward_copy(h, step).wait()
        for k in range(n_mp):
            for t in range(3):
                part = frecv[h, k, :qrows, t * 128 : (t + 1) * 128]
                low_row = (k % 2) * qrows
                stage[2 * t + k // 2, low_row : low_row + qrows, :] = part.astype(F32)

    def sweep(h, *passes):
        @pl.loop(0, pairs // GROUP)
        def _(i):
            for run in passes:
                run(h, i)

    collect(0)
    sweep(0, redo, weight_grads, input_grads)
    sweep(1, redo)
    if fused:
        end_second(last - 1)
    collect(1)
    sweep(1, weight_grads)
    if fused:
        part_out[:PARTS_EARLY] = small[: 16 * PARTS_EARLY, :].astype(BF).reshape(PARTS_EARLY, 16, units)

        def part_copy(step):
            other = lax.rem(mine + step, devices)
            return remote(part_out.at[other], part_in.at[step], part_sem, step, device(other))

        def whole_copy(step):
            other = lax.rem(mine + step, devices)
            return remote(part_out.at[mine], whole_in.at[mine], whole_sem, step, device(other))

        @pl.loop(1, devices)
        def _(step):
            @pl.when(lax.rem(mine + step, devices) < PARTS_EARLY)
            def _():
                part_copy(step).start()

        end_first(last)
    sweep(1, input_grads)
    share_stats(1)
    frame = []
    for acc in (acc_g, acc_b):
        column = jnp.broadcast_to(jnp.sum(acc[...], 1, keepdims=True), (local, 128))
        column = jnp.concatenate([column, jnp.zeros((256 - local, 128), F32)], 0)
        values = jnp.concatenate([jnp.transpose(column)[:SUB], jnp.zeros((SUB, 128), F32)], 1)
        values = jnp.where(odd > 0, pltpu.roll(values, local, 1), values)[:1]
        for i in range(n_mp // 2):
            frame.append(jnp.where(me // 2 == i, values, 0.0))
    if fused:
        frame = jnp.concatenate(frame + [jnp.zeros((12, units), F32)], 0)
        part_out[devices - n_mp + me] = frame.astype(BF)
        late_step = devices - n_mp - n_mp * dp

        @pl.when(dp < n_dp - 1)
        def _():
            part_copy(late_step).start()

        end_second(last)
        for step in range(last):
            zu_copy(step).wait()
        gu = [gbuf[0, z, x, i, c].astype(F32) for i in range(2)]
        for step in range(last):
            gu = [gu[i] + zu_in[step, i].astype(F32) for i in range(2)]
        y_out[...] = jnp.where(y > 0, gu[0], gu[1]).astype(BF)
        last_copy = remote(y_out, yu_in, y2_sem, 0, at(z, x, 1 - y, c))
        last_copy.start()
        cu_out[...] = jnp.where(y > 0, gu[1], gu[0])
        for step in range(last):
            zd_copy(step).wait()
        gd = gbuf[1, z, x, y, c].astype(F32)
        for step in range(last):
            gd = gd + zd_in[step].astype(F32)
        cd_out[...] = gd
    else:
        small[416:420, :] = jnp.concatenate(frame, 0)

    wait_stats(1)
    sums = [stat_in[1, k] for k in range(n_mp)]
    stat_out[...] = (sums[0] + sums[1] + sums[2] + sums[3]) * (1.0 / width)

    for h in range(2):

        @pl.loop(0, chunk)
        def _(i):
            b = h * chunk + lax.rem(i, 2) * pairs + i // 2
            one = stat_out[pl.ds(b, 1), :]
            two = stat_out[pl.ds(images + b, 1), :]
            first = pl.multiple_of(i * local, local)
            kept = cd[pl.ds(first, local), 256 * h : 256 * h + patches].astype(F32)
            grad = kept - mean_inv[1, pl.ds(b, 1), :] * (one + norm_of(b) * two)
            img[b] = grad.astype(BF)

    image_out = pltpu.make_async_copy(img, gi_hbm, out_sem.at[3])
    image_out.start()
    if fused:
        @pl.loop(1, devices)
        def _(step):
            other = lax.rem(mine + step, devices)

            @pl.when((other < PARTS_EARLY) | ((step == late_step) & (dp < n_dp - 1)))
            def _():
                part_copy(step).wait_send()

        @pl.when(mine < PARTS_EARLY)
        def _():
            @pl.loop(1, devices)
            def _(step):
                part_copy(step).wait_recv()

            total = part_out[mine].astype(F32)
            for step in range(1, devices):
                total = total + part_in[step].astype(F32)
            part_out[mine] = total.astype(BF)

        @pl.when(dp == n_dp - 1)
        def _():
            total = part_out[mine].astype(F32)
            for k in range(1, n_dp):
                part_copy(k * n_mp).wait_recv()
                total = total + part_in[k * n_mp].astype(F32)
            part_out[mine] = total.astype(BF)

        @pl.loop(1, devices)
        def _(step):
            whole_copy(step).start()

        whole_in[mine] = part_out[mine]
        last_copy.wait()
        cu_out[...] += yu_in[...].astype(F32)

        @pl.loop(1, devices)
        def _(step):
            whole_copy(step).wait()

        sums_out[...] = whole_in[...]
    else:
        small_out[...] = small[...]
        grad_out.wait()
    out_copy(1).wait()
    image_out.wait()


def unpack(
    bo_in, gi_in, sums, cu_in, cd_in,
    bo_out, gi_out, pg_out, pb_out, tu_out, tub_out, td_out, tdb_out, mg_out, mb_out,
    cu_out, cub_out, cd_out, cdb_out, small, bo, gi, cu, cd, sem,
):
    arrays = ((bo_in, bo_out, bo), (gi_in, gi_out, gi), (cu_in, cu_out, cu), (cd_in, cd_out, cd))
    arrivals, departures = [], []
    for i, (src, dst, held) in enumerate(arrays):
        count = held.shape[0]
        parts = PARTS if i < 2 else 1
        for part in range(parts):
            first, end = count * part // parts, count * (part + 1) // parts
            if i >= 2:
                first, end = 0, count
            rows = pl.ds(first, end - first)
            number = len(arrivals)
            arrivals.append(pltpu.make_async_copy(src.at[rows], held.at[rows], sem.at[0, number]))
            departures.append(pltpu.make_async_copy(held.at[rows], dst.at[rows], sem.at[1, number]))
    for copy in arrivals:
        copy.start()
    patches = tu_out.shape[0]
    small[...] = sums[...].astype(F32).reshape(small.shape)
    tu_out[...] = small[:patches, :]
    td_out[...] = small[200 : 200 + patches, :]

    def take(ref, first):
        count = ref.shape[0] // 384
        values = [small[first + i : first + i + 1, :] for i in range(count)]
        ref[...] = jnp.concatenate(values, 1).reshape(ref.shape)

    take(cub_out, 400)
    take(mg_out, 408)
    take(mb_out, 410)
    take(cdb_out, 412)
    take(tub_out, 414)
    tdb_out[...] = small[415:416, :patches].reshape(tdb_out.shape)
    for ref, first in ((pg_out, 448), (pb_out, 450)):
        values = [
            sum(small[first + 16 * k + i : first + 16 * k + i + 1, :] for k in range(4)) for i in range(2)
        ]
        ref[...] = jnp.concatenate(values, 1).reshape(ref.shape)
    for arrival, departure in zip(arrivals, departures):
        arrival.wait()
        departure.start()
    for departure in departures:
        departure.wait()


def shards(
    axes, images, counts, pre_gain, pre_bias, token_up, token_up_bias, token_down, token_down_bias,
    mid_gain, mid_bias, channel_up, channel_up_bias, channel_down, channel_down_bias, cotangent,
):
    n_dp, n_mp = axes
    count, patches, local = images.shape
    width, hidden = channel_up.shape
    units = token_up.shape[1]
    quarter = cotangent.shape[1]
    chunk = count // 2
    rows = quarter * chunk
    qpad = -(-quarter * SUB // 16) * 16
    fused = n_dp == 8 and n_mp == 4 and hidden == 4 * width
    unit = hidden // 32
    vector = [jax.ShapeDtypeStruct((n,), F32) for n in (width, hidden, units, patches)]
    table = jax.ShapeDtypeStruct((patches, units), F32)
    any_space = pl.BlockSpec(memory_space=pl.ANY)
    vmem = pl.BlockSpec(memory_space=pltpu.VMEM)
    smem = pl.BlockSpec(memory_space=pltpu.SMEM)
    V = pltpu.VMEM
    dma = pltpu.SemaphoreType.DMA
    if fused:
        slab = jax.ShapeDtypeStruct((unit, width), F32)
        grads = (jax.ShapeDtypeStruct((32, 16, units), BF), slab, slab)
        grad_specs = (vmem,) * 3
    else:
        grads = (
            jax.ShapeDtypeStruct((2, hidden // width, 2, 2, 2, unit, width), BF),
            jax.ShapeDtypeStruct((512, units), F32),
        )
        grad_specs = (any_space, vmem)
    pair = dma((2, n_mp - 1))
    extra = [
        V((2, 2, 2, unit, width), BF),
        V((4, 2, unit, width), BF),
        V((4, 2, unit, width), BF),
        V((4, unit, width), BF),
        V((3, 2, unit, width), BF),
        V((3, unit, width), BF),
        V((unit, width), BF),
        V((unit, width), BF),
        V((32, 16, units), BF),
        V((32, 16, units), BF),
        V((32, 16, units), BF),
        dma((2, 1)),
        dma((2, 4)),
        dma((2, 4)),
        dma((2, 4)),
        dma((2, 3)),
        dma((2, 3)),
        dma((2, 1)),
        dma((2, 32)),
        dma((2, 32)),
        pltpu.SemaphoreType.REGULAR,
    ]
    out = pl.pallas_call(
        functools.partial(kernel, axes, fused),
        out_shape=(
            jax.ShapeDtypeStruct((quarter, count, width), BF),
            jax.ShapeDtypeStruct((count, local, patches), BF),
        )
        + grads,
        in_specs=[smem] + [any_space] * 4 + [vmem] * 10,
        out_specs=(any_space, any_space) + grad_specs,
        scratch_shapes=[
            V((count, local, patches), BF),
            V((width, hidden), BF),
            V((hidden, width), BF),
            V((3, quarter, chunk, width), BF),
            V((hidden // width, rows, width), BF),
            V((hidden // width, rows - width, width), BF),
            V((2 * count, patches), F32),
            V((2, n_mp, 2 * count, patches), F32),
            V((2, count, patches), F32),
            V((GROUP, 2 * local, units), BF),
            V((width // 128, rows, 128), F32),
            V((2, n_mp, qpad, 2 * local), BF),
            V((2, n_mp, qpad, 2 * local), BF),
            V((rows, width), BF),
            V((2, quarter, chunk, width), BF),
            V((rows, width), F32),
            V((2, hidden // width, 2, 2, 2, unit, width), BF),
            V((local, patches), F32),
            V((local, patches), F32),
            V((SUB, hidden), F32),
            V((512, units), F32),
            V((local, 128), F32),
            V((local, 128), F32),
            dma((5,)),
            dma((4,)),
            pair,
            pair,
            pair,
            pair,
            pair,
            pair,
            pltpu.SemaphoreType.REGULAR((2,)),
        ]
        + (extra if fused else []),
        compiler_params=pltpu.CompilerParams(
            collective_id=0, has_side_effects=True, vmem_limit_bytes=64 * 2**20 - 2**17
        ),
    )(
        counts,
        jnp.transpose(images, (0, 2, 1)),
        jnp.transpose(cotangent, (1, 0, 2)),
        channel_up,
        channel_down,
        token_up,
        jnp.transpose(token_down),
        pre_gain,
        pre_bias,
        token_up_bias,
        token_down_bias,
        mid_gain,
        mid_bias,
        channel_up_bias,
        channel_down_bias,
    )
    if fused:
        finals = list(vector[:1] * 2 + [table, vector[2], table, vector[3]] + vector[:1] * 2)
        finals += [slab, vector[1], slab, vector[0]]
        rest = pl.pallas_call(
            unpack,
            out_shape=tuple(jax.ShapeDtypeStruct(o.shape, o.dtype) for o in out[:2]) + tuple(finals),
            in_specs=[any_space] * 2 + [vmem] + [any_space] * 2,
            out_specs=(any_space, any_space) + (vmem,) * 8 + (any_space, vmem, any_space, vmem),
            scratch_shapes=[V((512, units), F32)]
            + [V(o.shape, o.dtype) for o in (*out[:2], *out[3:])]
            + [dma((2, 2 * PARTS + 2))],
            compiler_params=pltpu.CompilerParams(vmem_limit_bytes=60 * 2**20),
        )(*out)
        rest = list(rest)
        rest[0] = jnp.transpose(rest[0], (1, 0, 2))
        rest[1] = jnp.transpose(rest[1], (0, 2, 1))
        rest[6] = jnp.transpose(rest[6])
        rest[10] = jnp.transpose(rest[10])
        return tuple(rest)
    block_out, grad_images = jnp.transpose(out[0], (1, 0, 2)), jnp.transpose(out[1], (0, 2, 1))
    both = ("dp", "mp")
    grads = out[2].reshape(2, hidden, width).astype(F32)
    wide = lax.psum_scatter(grads, both, scatter_dimension=1, tiled=True)
    small = lax.psum(out[3], both)
    return (
        block_out,
        grad_images,
        small[416:418].reshape(width),
        small[418:420].reshape(width),
        small[:patches],
        small[414],
        jnp.transpose(small[200 : 200 + patches]),
        small[415, :patches],
        small[408:410].reshape(width),
        small[410:412].reshape(width),
        jnp.transpose(wide[0]),
        small[400:408].reshape(hidden),
        wide[1],
        small[412:414].reshape(width),
    )


def solution(mesh):
    axes = (mesh.shape["dp"], mesh.shape["mp"])
    in_specs = (P("dp", None, "mp"), P("dp")) + (P(),) * 12 + (P("dp", "mp", None),)
    out_specs = (
        (P("dp", "mp", None), P("dp", None, "mp"))
        + (P(),) * 8
        + (P(None, ("dp", "mp")), P(), P(("dp", "mp"), None), P())
    )
    return jax.shard_map(
        functools.partial(shards, axes), mesh=mesh, in_specs=in_specs, out_specs=out_specs, check_vma=False
    )
```
